256 devices in a mesh: ctx: 32 (over z, x), tp: 8 (over y, core).
Axes of the slice: x: 4, y: 4, z: 8, core: 2. Of those that a mesh axis runs over, the one named last changes fastest.
Arguments:
- mixer_input: bfloat16 [8192, 16384], P('ctx', 'tp'), may hold values from -6 to 6
- gate_input: bfloat16 [8192, 16384], P('ctx', 'tp'), may hold values from -6 to 6
- input_map: bfloat16 [8192, 2048], P('ctx', 'tp'), may hold values from -2 to 2
- output_map: bfloat16 [8192, 2048], P('ctx', 'tp'), may hold values from -2 to 2
- step_raw: float32 [256, 8192], P('tp', 'ctx'), may hold values from -4 to 4
- step_bias: float32 [256], P('tp'), may hold values from -4 to -1
- decay_log: float32 [256], P('tp'), may hold values from -7 to 0.7
- skip_gain: float32 [256], P('tp'), may hold values from 0.1 to 1.9
- norm_gain: float32 [16384], P('tp'), may hold values from 0.1 to 1.9
- queries: bfloat16 [8192, 8192], P('ctx', 'tp'), may hold values from -6 to 6
- key_heads: bfloat16 [8192, 1024], P('ctx', 'tp'), may hold values from -6 to 6
- value_heads: bfloat16 [8192, 1024], P('ctx', 'tp'), may hold values from -6 to 6
- out_weight: bfloat16 [8192, 4096], P('tp'), may hold values from -0.0625 to 0.0625
- rollout_lengths: int32 [4], replicated, may hold values from 1 to 4096, 8192 in all
Outputs:
- mamba_out: bfloat16 [8192, 16384], P('ctx', 'tp')
- block_out: bfloat16 [8192, 4096], P('ctx', 'tp')
The draws below stay inside these ranges and needn't reach their ends.
Inputs may be any that keep to these rules, and one draw needn't show every extreme that they name: `rollout_lengths`: the longest rollout has exactly 4096 tokens; the lengths sum to 8192.
All inputs are finite; a program needn't handle non-finite values.
Results may differ from the reference program's by a relative error of at most 0.0075.
Values may be sent and summed in bfloat16 or wider, within the bound.
No kernel may reach another device: no remote copies, remote signals or barrier semaphores. Data moves between devices by JAX's collectives and lax.ppermute only.
A program may use at most 192 MiB of HBM per device.

```python
import math
import jax
import jax.numpy as jnp
import numpy as np
from jax import lax

HEADS = 256
HEAD_P = 64
STATE = 256
GROUPS = 8
QHEADS = 64
KVHEADS = 8
HEAD_DIM = 128
OUT_COLS = 4096
SPAN = 128
ROLLOUTS = 4
TOKENS = 8192
MOST = 4096


def draw_queries(key, part):
    own = jax.random.fold_in(key, 11)
    base = jnp.clip(1.8 * jax.random.normal(own, (TOKENS, QHEADS * HEAD_DIM), jnp.float32), -6.0, 6.0)
    return base.astype(jnp.bfloat16)


def draw_key_heads(key, part):
    own = jax.random.fold_in(key, 13)
    base = jnp.clip(1.8 * jax.random.normal(own, (TOKENS, KVHEADS * HEAD_DIM), jnp.float32), -6.0, 6.0)
    return base.astype(jnp.bfloat16)


def shard_levels(stream_key, extent, pieces, least, top_value):
    def one(axis_at, blocks):
        draws = jax.random.uniform(jax.random.fold_in(jax.random.fold_in(stream_key, 6), axis_at), (blocks,), jnp.float32, least / len(pieces), top_value / len(pieces))
        return jnp.repeat(jnp.exp(draws), extent[axis_at] // blocks).reshape((-1,) + (1,) * (len(extent) - axis_at - 1))

    gain = one(*pieces[0])
    for cut in pieces[1:]:
        gain = gain * one(*cut)
    return gain


def split_up(number_of, total, bound, lean):
    weights = [(1 << 20) // math.isqrt(rank ** lean) + 1 for rank in range(2, number_of + 1)]
    surplus, holding = total - bound - (number_of - 1), [1] * (number_of - 1)
    while surplus > 0:
        free = [i for i in range(number_of - 1) if holding[i] < bound]
        whole, remaining = sum([weights[i] for i in free]), surplus
        for i in free:
            addition = min(bound - holding[i], max(1, remaining * weights[i] // whole), surplus)
            holding[i] = holding[i] + addition
            surplus = surplus - addition
    return np.array([bound] + holding)


def ragged_sizes(stream_key, count, total, reach, slope):
    if count == 2:
        one = jax.random.randint(stream_key, (), max(1, total - reach), min(reach, total - 1) + 1)
        return jnp.stack([one, total - one])
    tallies = jnp.asarray(split_up(count, total, reach, slope), jnp.int32)
    couples = (count - 1) // 2
    giver, taker = tallies[1:1 + 2 * couples:2], tallies[2:2 + 2 * couples:2]
    slack = jnp.minimum(giver - 1, reach - taker)
    passed = jax.random.randint(jax.random.fold_in(stream_key, 1), (couples,), 0, 1 << 20) % (slack + 1)
    tallies = tallies.at[1:1 + 2 * couples:2].set(giver - passed).at[2:2 + 2 * couples:2].set(taker + passed)
    return tallies[jax.random.permutation(jax.random.fold_in(stream_key, 2), count)]


def centred(own_key, shape, deviation, reach, pieces=(), kind=jnp.bfloat16):
    drawn = jax.random.normal(own_key, shape, jnp.float32) * deviation
    if len(pieces) > 0:
        drawn = shard_levels(own_key, shape, pieces, -0.22, 0.18) * drawn
    return jnp.clip(drawn, min=-reach, max=reach).astype(kind)


def setup_inputs(seed: int = 0) -> dict:
    keys = jax.random.split(jax.random.key(seed), 15)
    mixer_input = centred(keys[0], (TOKENS, HEADS * HEAD_P), 1.0, 6.0, ((0, 32), (1, 8)))
    gate_input = centred(keys[1], (TOKENS, HEADS * HEAD_P), 1.0, 6.0, ((0, 32), (1, 8)))
    input_map = centred(keys[2], (TOKENS, GROUPS * STATE), 0.3, 2.0, ((0, 32), (1, 8)))
    output_map = centred(keys[3], (TOKENS, GROUPS * STATE), 0.3, 2.0, ((0, 32), (1, 8)))
    step_raw = centred(keys[4], (HEADS, TOKENS), 1.0, 4.0, ((0, 8), (1, 32)), jnp.float32)
    step_bias = jnp.clip(-4.0 + 3.0 * jax.random.uniform(keys[5], (HEADS,), jnp.float32) ** shard_levels(keys[5], (HEADS,), ((0, 8),), -0.2, 0.2), -4.0, -1.0)
    decay_log = jnp.clip(-7.0 + 7.7 * jax.random.uniform(keys[6], (HEADS,), jnp.float32) ** shard_levels(keys[6], (HEADS,), ((0, 8),), -0.2, 0.2), -7.0, 0.7)
    skip_gain = jnp.clip(1.0 + 0.18 * jax.random.normal(keys[7], (HEADS,), jnp.float32), 0.1, 1.9)
    norm_gain = jnp.clip(1.0 + 0.18 * jax.random.normal(keys[8], (HEADS * HEAD_P,), jnp.float32), 0.1, 1.9)
    queries = draw_queries(jax.random.fold_in(keys[14], 71), 0)
    key_heads = draw_key_heads(jax.random.fold_in(keys[14], 71), 0)
    value_heads = centred(keys[11], (TOKENS, KVHEADS * HEAD_DIM), 1.0, 6.0, ((0, 32), (1, 8)))
    out_weight = centred(keys[12], (QHEADS * HEAD_DIM, OUT_COLS), (QHEADS * HEAD_DIM) ** -0.5, 0.0625, ((0, 8),))
    rollout_lengths = ragged_sizes(keys[13], ROLLOUTS, TOKENS, MOST, 2).astype(jnp.int32)
    return {"mixer_input": mixer_input, "gate_input": gate_input, "input_map": input_map, "output_map": output_map, "step_raw": step_raw, "step_bias": step_bias, "decay_log": decay_log, "skip_gain": skip_gain, "norm_gain": norm_gain, "queries": queries, "key_heads": key_heads, "value_heads": value_heads, "out_weight": out_weight, "rollout_lengths": rollout_lengths}


norm_eps = 1e-05
big_negative = -1e+30

def rollout_of(index, lengths):
    ends = jnp.cumsum(lengths).astype(jnp.int32)
    counted = lax.optimization_barrier(jnp.sum((index[:, None] >= ends[None, :]).astype(jnp.int32), axis=1))
    return jnp.where(index < 0, jnp.int32(-1), counted).astype(jnp.int32)

def span_step(state, parts):
    mixer_block, in_block, out_block, width_block, rate_block, seg_block, seg_prev = parts
    heads_all, state_dim, head_width = state.shape
    span_len = mixer_block.shape[0]
    groups_all = in_block.shape[1] // state_dim
    per_group = heads_all // groups_all
    cum = jnp.cumsum(rate_block, axis=1)
    order = jnp.arange(span_len)
    same = (seg_block[:, None] == seg_block[None, :]) & (order[:, None] >= order[None, :])
    diff = cum[:, :, None] - cum[:, None, :]
    decay = jnp.where(same[None], jnp.exp(jnp.where(same[None], diff, 0.0)), 0.0)
    in_g = in_block.reshape(span_len, groups_all, state_dim).astype(jnp.float32)
    out_g = out_block.reshape(span_len, groups_all, state_dim).astype(jnp.float32)
    inner = jnp.einsum('ign,jgn->gij', out_g, in_g)
    mix = (decay.reshape(groups_all, per_group, span_len, span_len) * inner[:, None] * width_block.reshape(groups_all, per_group, 1, span_len)).astype(jnp.bfloat16)
    mixer_g = mixer_block.reshape(span_len, groups_all, per_group, head_width).astype(jnp.float32)
    result = jnp.einsum('gkij,jgkp->igkp', mix.astype(jnp.float32), mixer_g)
    kept = (seg_block == seg_prev).astype(jnp.float32)
    lead = (jnp.exp(cum) * kept[None, :]).T.reshape(span_len, groups_all, per_group, 1)
    carried = jnp.einsum('ign,gknp->igkp', out_g, state.reshape(groups_all, per_group, state_dim, head_width), precision=lax.Precision.HIGHEST)
    result = result + lead * carried
    last = cum[:, -1]
    tail = jnp.where((seg_block == seg_block[-1])[None, :], jnp.exp(last[:, None] - cum), 0.0) * width_block
    feed = (in_g[:, :, None, :] * tail.reshape(groups_all, per_group, span_len).transpose(2, 0, 1)[..., None]).astype(jnp.bfloat16)
    fresh = jnp.einsum('sgkn,sgkp->gknp', feed.astype(jnp.float32), mixer_g).reshape(heads_all, state_dim, head_width)
    through = jnp.where(seg_block[-1] == seg_prev, jnp.exp(last), 0.0)
    return (through[:, None, None] * state + fresh, result.reshape(span_len, heads_all * head_width))

def mamba_part(mixer_input, gate_input, input_map, output_map, step_raw, step_bias, decay_log, skip_gain, norm_gain, rollout):
    tokens_all = mixer_input.shape[0]
    heads_all = step_raw.shape[0]
    width = jax.nn.softplus(step_raw + step_bias[:, None])
    rate = -jnp.exp(decay_log)[:, None] * width
    count = tokens_all // SPAN
    seg_blocks = rollout.reshape(count, SPAN)
    seg_prev = jnp.concatenate([jnp.array([-1], jnp.int32), seg_blocks[:-1, -1]]).astype(jnp.int32)
    parts = (mixer_input.reshape(count, SPAN, -1), input_map.reshape(count, SPAN, -1), output_map.reshape(count, SPAN, -1), width.reshape(heads_all, count, SPAN).transpose(1, 0, 2), rate.reshape(heads_all, count, SPAN).transpose(1, 0, 2), seg_blocks, seg_prev)
    start_state = jnp.zeros((heads_all, STATE, HEAD_P), jnp.float32)
    ignored, blocks = lax.scan(span_step, start_state, parts)
    mixed = blocks.reshape(tokens_all, heads_all, HEAD_P) + skip_gain[None, :, None] * mixer_input.reshape(tokens_all, heads_all, HEAD_P).astype(jnp.float32)
    gated = mixed.reshape(tokens_all, heads_all * HEAD_P) * jax.nn.silu(gate_input.astype(jnp.float32))
    grouped = gated.reshape(tokens_all, GROUPS, -1)
    factor = lax.rsqrt(lax.optimization_barrier(jnp.mean(grouped * grouped, axis=2, keepdims=True)) + norm_eps)
    return ((grouped * factor).reshape(tokens_all, -1) * norm_gain[None, :]).astype(jnp.bfloat16)

def attend_head(query_head, key_head, value_head, rollout):
    tokens_all = query_head.shape[0]
    block = math.gcd(tokens_all, 512)
    positions = jnp.arange(tokens_all, dtype=jnp.int32)
    scale = 1.0 / math.sqrt(HEAD_DIM)
    key_f = key_head.astype(jnp.float32)
    value_f = value_head.astype(jnp.float32)

    def one_block(items):
        query_block, query_pos, query_roll = items
        logits = jnp.einsum('tgd,sd->gts', query_block.astype(jnp.float32), key_f) * scale
        visible = (query_roll[:, None] == rollout[None, :]) & (query_pos[:, None] >= positions[None, :])
        masked = jnp.where(visible[None], logits, big_negative)
        peak = lax.optimization_barrier(jnp.max(masked, axis=2, keepdims=True))
        weights = jnp.where(visible[None], jnp.exp(masked - peak), 0.0)
        total = lax.optimization_barrier(jnp.sum(weights, axis=2))
        probs = weights.astype(jnp.bfloat16)
        summed = jnp.einsum('gts,sd->tgd', probs.astype(jnp.float32), value_f)
        return summed / total.T[:, :, None]
    count = tokens_all // block
    outputs = lax.map(one_block, (query_head.reshape(count, block, query_head.shape[1], query_head.shape[2]), positions.reshape(count, block), rollout.reshape(count, block)))
    return outputs.reshape(tokens_all, query_head.shape[1], query_head.shape[2])

def reference(mixer_input, gate_input, input_map, output_map, step_raw, step_bias, decay_log, skip_gain, norm_gain, queries, key_heads, value_heads, out_weight, rollout_lengths):
    tokens_all = mixer_input.shape[0]
    rollout = rollout_of(jnp.arange(tokens_all, dtype=jnp.int32), rollout_lengths)
    mamba_out = mamba_part(mixer_input, gate_input, input_map, output_map, step_raw, step_bias, decay_log, skip_gain, norm_gain, rollout)
    group_size = QHEADS // KVHEADS
    query_split = queries.reshape(tokens_all, KVHEADS, group_size, HEAD_DIM).transpose(1, 0, 2, 3)
    key_split = key_heads.reshape(tokens_all, KVHEADS, HEAD_DIM).transpose(1, 0, 2)
    value_split = value_heads.reshape(tokens_all, KVHEADS, HEAD_DIM).transpose(1, 0, 2)

    def per_head(items):
        return attend_head(items[0], items[1], items[2], rollout)
    heads_out = lax.map(per_head, (query_split, key_split, value_split))
    attended = heads_out.transpose(1, 0, 2, 3).reshape(tokens_all, QHEADS * HEAD_DIM).astype(jnp.bfloat16)
    block_out = jnp.dot(attended, out_weight, preferred_element_type=jnp.float32).astype(jnp.bfloat16)
    return (mamba_out, block_out)
```

```python
import math

import jax
import jax.numpy as jnp
from jax import lax
from jax.experimental import pallas as pl
from jax.experimental.pallas import tpu as pltpu
from jax.sharding import PartitionSpec as P

HEAD_P = 64
STATE = 256
HEAD_DIM = 128
NZ = 8
NX = 4
NY = 4
LOG2E = math.log2(math.e)
EPS = 1e-05
BIG = -1e30
F32 = jnp.float32
BF16 = jnp.bfloat16
EXTRA = 16
QUARTER = 512


def iota(shape, dim):
    return lax.broadcasted_iota(jnp.int32, shape, dim)


def split3(a):
    hi = a.astype(BF16)
    rest = a - hi.astype(F32)
    mid = rest.astype(BF16)
    low = (rest - mid.astype(F32)).astype(BF16)
    return hi, mid, low


def spread(a, expand, terms=3):
    total = None
    for part in split3(a)[:terms]:
        one = jnp.dot(part, expand, preferred_element_type=F32)
        total = one if total is None else total + one
    return total


def expander(heads, lanes):
    return (iota((heads, lanes), 1) // HEAD_P == iota((heads, lanes), 0)).astype(F32).astype(BF16)


def ends_of(lengths):
    e0 = lengths[0]
    e1 = e0 + lengths[1]
    e2 = e1 + lengths[2]
    return e0, e1, e2, e2 + lengths[3]


def rollout_at(pos, ends):
    count = jnp.zeros_like(pos)
    for e in ends:
        count = count + (pos >= e).astype(jnp.int32)
    return jnp.where(pos < 0, -1, count)


def state_kernel(place, lengths, x_ref, b_ref, raw_ref, bias_ref, alog_ref,
                 o0, o1, o2, o3, d_ref, cumt_ref, lead_ref, scr):
    heads, toks = raw_ref.shape
    lanes = x_ref.shape[1]
    zi, xi = place[0], place[1]
    first = (zi * NX + xi) * toks
    ends = ends_of(lengths)
    width = jax.nn.softplus(raw_ref[...] + bias_ref[...])
    rate2 = (-LOG2E * jnp.exp(alog_ref[...])) * width
    upper = (iota((toks, toks), 0) <= iota((toks, toks), 1)).astype(F32)
    cum = jnp.dot(rate2, upper, precision=lax.Precision.HIGHEST, preferred_element_type=F32)
    cumt = cum.T
    width_t = width.T
    d_ref[...] = cum - jnp.log2(width)
    cumt_ref[...] = cumt
    before = rollout_at(first - 1, ends)
    last = rollout_at(first + (toks - 1), ends)
    roll = rollout_at(first + iota((toks, heads), 0), ends)
    lead_ref[...] = jnp.where(roll == before, jnp.exp2(cumt), 0.0)
    end = cumt[toks - 1:toks, :]
    tail = jnp.where(roll == last, jnp.exp2(end - cumt), 0.0) * width_t
    expand = expander(heads, lanes)
    xw = (spread(tail, expand, 2) * x_ref[...].astype(F32)).astype(BF16)
    state = lax.dot_general(b_ref[...], xw, (((0,), (0,)), ((), ())), preferred_element_type=F32)
    through = jnp.where(last == before, jnp.exp2(end), 0.0)
    th = [jnp.dot(part, expand, preferred_element_type=F32) for part in split3(through)]
    row = iota((EXTRA, lanes), 0)
    extra = jnp.where(row == 0, th[0], jnp.where(row == 1, th[1], jnp.where(row == 2, th[2], 0.0)))
    whole = jnp.concatenate([state, extra], axis=0).astype(BF16)
    for q in range(NX):
        scr[q] = whole[:, q * QUARTER:(q + 1) * QUARTER]
    for k, out in enumerate((o0, o1, o2, o3)):
        out[...] = scr[lax.rem(xi + k, NX)]


def row_kernel(place, a0, a1, a2, a3, p_ref, t_ref, pth_ref, th_ref, scr):
    xi = place[1]
    for k, a in enumerate((a0, a1, a2, a3)):
        scr[lax.rem(xi - k + NX, NX)] = a[...]
    total = jnp.zeros((STATE, QUARTER), F32)
    through = jnp.ones((1, QUARTER), F32)
    for j in range(NX):
        p_ref[j] = total.astype(BF16)
        pth_ref[j] = jnp.broadcast_to(through, (8, QUARTER))
        tail = scr[j, STATE:STATE + EXTRA, :].astype(F32)
        one = tail[0:1] + tail[1:2] + tail[2:3]
        total = one * total + scr[j, :STATE, :].astype(F32)
        through = through * one
    t_ref[...] = total.astype(BF16)
    th_ref[...] = jnp.broadcast_to(through, (8, QUARTER))


def back_kernel(place, p_ref, pth_ref, r_ref, o0, o1, o2, o3):
    xi = place[1]
    came = r_ref[...].astype(F32)
    for k, out in enumerate((o0, o1, o2, o3)):
        j = lax.rem(xi + k, NX)
        out[...] = (p_ref[j].astype(F32) + pth_ref[j][0:1] * came).astype(BF16)


def local_kernel(place, lengths, x_ref, b_ref, c_ref, d_ref, cumt_ref, skip_ref, y_ref):
    toks, lanes = x_ref.shape
    heads = d_ref.shape[0]
    half = toks // 2
    first = (place[0] * NX + place[1]) * toks
    ends = ends_of(lengths)
    roll_t = rollout_at(first + iota((toks, toks), 0), ends)
    roll_s = rollout_at(first + iota((toks, toks), 1), ends)
    seen = (roll_t == roll_s) & (iota((toks, toks), 0) >= iota((toks, toks), 1))
    inner = lax.dot_general(c_ref[...], b_ref[...], (((1,), (1,)), ((), ())), preferred_element_type=F32)
    inner = jnp.where(seen, inner, 0.0)
    left = iota((half, 128), 1) < HEAD_P
    skip = spread(skip_ref[...], expander(heads, lanes))
    d_all = d_ref[...]
    cumt = cumt_ref[...]
    for pair in range(heads // 2):
        cols = slice(pair * 128, (pair + 1) * 128)
        x_pair = x_ref[:, cols]
        for rows, width in ((slice(0, half), half), (slice(half, toks), toks)):
            res = []
            for h in (2 * pair, 2 * pair + 1):
                diff = cumt[rows, h:h + 1] - d_all[h:h + 1, :width]
                mix = (jnp.exp2(jnp.minimum(diff, 64.0)) * inner[rows, :width]).astype(BF16)
                res.append(jnp.dot(mix, x_pair[:width], preferred_element_type=F32))
            y_ref[rows, cols] = jnp.where(left, res[0], res[1]) + skip[:, cols] * x_pair[rows].astype(F32)


def gate_kernel(place, y_ref, c_ref, lead_ref, gate_ref, gain_ref, i0, i1, i2, i3, out_ref, scr):
    toks, lanes = y_ref.shape
    heads = lead_ref.shape[1]
    xi = place[1]
    for k, a in enumerate((i0, i1, i2, i3)):
        scr[lax.rem(xi - k + NX, NX)] = a[...]
    expand = expander(heads, lanes)
    square = jnp.zeros((toks, 1), F32)
    held = []
    for q in range(NX):
        cols = slice(q * QUARTER, (q + 1) * QUARTER)
        carried = jnp.dot(c_ref[...], scr[q], preferred_element_type=F32)
        lead = spread(lead_ref[...], expand[:, cols], 2)
        v = gate_ref[:, cols].astype(F32)
        gated = (y_ref[:, cols] + lead * carried) * (v / (1.0 + jnp.exp(-v)))
        square = square + jnp.sum(gated * gated, axis=1, keepdims=True)
        held.append(gated)
    factor = lax.rsqrt(square * (1.0 / lanes) + EPS)
    for q in range(NX):
        cols = slice(q * QUARTER, (q + 1) * QUARTER)
        out_ref[:, cols] = (held[q] * factor * gain_ref[:, cols]).astype(BF16)


def attend_kernel(place, lengths, q_ref, own, z1, z2, z3, z4, g1, g2, g3, out_ref,
                  k_buf, v_buf, q_buf, s_a, s_b):
    toks = q_ref.shape[0]
    heads = q_ref.shape[1] // HEAD_DIM
    chunks = k_buf.shape[0]
    zi, xi = place[0], place[1]
    first = (zi * NX + xi) * toks
    ends = ends_of(lengths)
    lane = iota((toks, HEAD_DIM), 1)
    ones = (lane == 0).astype(F32).astype(BF16)

    def put(slot, kv):
        k_buf[slot, :, :HEAD_DIM] = kv[:, :HEAD_DIM]
        v_buf[slot, :, :HEAD_DIM] = kv[:, HEAD_DIM:]

    put(16, own)
    for r, a in ((1, z1), (2, z2), (3, z3), (4, z4)):
        put(16 - 4 * r, a)
    for k, g in ((1, g1), (2, g2), (3, g3)):
        ahead = xi >= k
        put(jnp.where(ahead, 16 - k, 4 - k), g[0:toks, :])
        for r in (1, 2, 3):
            put(jnp.where(ahead, 16 - 4 * r - k, 20 - 4 * r - k), g[r * toks:(r + 1) * toks, :])
    for j in range(chunks):
        pos = first + (j - (chunks - 1)) * toks + iota((toks, HEAD_DIM), 0)
        k_buf[j, :, HEAD_DIM:] = jnp.where(rollout_at(pos, ends) == lane, 0.0, BIG).astype(BF16)
        v_buf[j, :, HEAD_DIM:] = ones
    mine = (rollout_at(first + iota((toks, HEAD_DIM), 0), ends) == lane).astype(F32).astype(BF16)
    for h in range(heads):
        q_buf[h, :, :HEAD_DIM] = q_ref[:, h * HEAD_DIM:(h + 1) * HEAD_DIM]
        q_buf[h, :, HEAD_DIM:] = mine
    causal = iota((toks, toks), 0) >= iota((toks, toks), 1)
    scale = LOG2E / math.sqrt(HEAD_DIM)

    def scores(h, buf, j, peak):
        s = lax.dot_general(q_buf[h], k_buf[j], (((1,), (1,)), ((), ())), preferred_element_type=F32)
        if j == chunks - 1:
            s = jnp.where(causal, s, BIG)
        buf[j] = s
        return jnp.maximum(peak, jnp.maximum(s[:, :128], s[:, 128:]))

    def finish(h, acc):
        res = acc[:, :HEAD_DIM] / acc[:, HEAD_DIM:HEAD_DIM + 1]
        out_ref[h] = res.astype(BF16)

    def weigh(buf, j, top):
        p = jnp.exp2((buf[j] - top) * scale).astype(BF16)
        return jnp.dot(p, v_buf[j], preferred_element_type=F32)

    low = jnp.full((toks, 128), BIG, F32)
    peak = low
    for j in range(chunks):
        peak = scores(0, s_a, j, peak)

    def both(h, buf_now, buf_next, peak):
        top = jnp.max(peak, axis=1, keepdims=True)
        nxt = jnp.minimum(h + 1, heads - 1)
        peak = low
        acc = jnp.zeros((toks, 2 * HEAD_DIM), F32)
        for j in range(chunks):
            peak = scores(nxt, buf_next, j, peak)
            acc = acc + weigh(buf_now, j, top)
        finish(h, acc)
        return peak

    def two(i, peak):
        peak = both(2 * i, s_a, s_b, peak)
        return both(2 * i + 1, s_b, s_a, peak)

    lax.fori_loop(0, heads // 2, two, peak)


def project_kernel(place, a_ref, w_ref, out_ref, wide):
    h = a_ref.shape[0]

    @pl.when(pl.program_id(0) == 0)
    def _():
        for i in range(h):
            wide[:, i * HEAD_DIM:(i + 1) * HEAD_DIM] = a_ref[i]

    out_ref[0] = jnp.dot(wide[...], w_ref[...], preferred_element_type=F32).astype(BF16)


def vmem(n):
    return [pl.BlockSpec(memory_space=pltpu.VMEM)] * n


def smem(n):
    return [pl.BlockSpec(memory_space=pltpu.SMEM)] * n


def sds(shape, dtype):
    return jax.ShapeDtypeStruct(shape, dtype)


PARAMS = pltpu.CompilerParams(vmem_limit_bytes=56 * 1024 * 1024)


def x_shift(k):
    return [(NX * z + x, NX * z + (x + k) % NX) for z in range(NZ) for x in range(NX)]


def y_shift(k):
    return [(2 * y + c, 2 * ((y + k) % NY) + c) for y in range(NY) for c in range(2)]


Z_STEP = [(NX * z + x, NX * (z + 1) + x) for z in range(NZ - 1) for x in range(NX)]
TWIN = [(i, i ^ 1) for i in range(2 * NY)]


def body(mixer_input, gate_input, input_map, output_map, step_raw, step_bias, decay_log, skip_gain,
         norm_gain, queries, key_heads, value_heads, out_weight, rollout_lengths):
    toks, lanes = mixer_input.shape
    heads = step_raw.shape[0]
    ctx = lax.axis_index("ctx")
    tp = lax.axis_index("tp")
    zi, xi = ctx // NX, ctx % NX
    place = jnp.stack([zi, xi, tp // 2, tp % 2]).astype(jnp.int32)
    msg = sds((STATE + EXTRA, QUARTER), BF16)
    quarter = sds((STATE, QUARTER), BF16)

    own = jnp.concatenate([key_heads, value_heads], axis=1)
    zs = [own]
    for _ in range(4):
        zs.append(lax.ppermute(zs[-1], "ctx", Z_STEP))

    o0, o1, o2, o3, dd, cumt, lead = pl.pallas_call(
        state_kernel,
        in_specs=smem(2) + vmem(5),
        out_specs=vmem(7),
        out_shape=[msg] * 4 + [sds((heads, toks), F32), sds((toks, heads), F32), sds((toks, heads), F32)],
        scratch_shapes=[pltpu.VMEM((NX, STATE + EXTRA, QUARTER), BF16)],
        compiler_params=PARAMS,
        name="chunk_states",
    )(place, rollout_lengths, mixer_input, input_map, step_raw, step_bias[:, None], decay_log[:, None])
    came = [o0] + [lax.ppermute(o, "ctx", x_shift(k)) for k, o in ((1, o1), (2, o2), (3, o3))]
    prefix, total, pth, th = pl.pallas_call(
        row_kernel,
        in_specs=smem(1) + vmem(4),
        out_specs=vmem(4),
        out_shape=[sds((NX, STATE, QUARTER), BF16), quarter, sds((NX, 8, QUARTER), F32), sds((8, QUARTER), F32)],
        scratch_shapes=[pltpu.VMEM((NX, STATE + EXTRA, QUARTER), BF16)],
        compiler_params=PARAMS,
        name="row_scan",
    )(place, *came)

    gs = []
    for k in (1, 2, 3):
        edge = jnp.where(xi + k < NX, own, zs[4])
        gs.append(lax.ppermute(jnp.concatenate([edge, zs[1], zs[2], zs[3]], axis=0), "ctx", x_shift(k)))

    carry = lax.ppermute(total, "ctx", Z_STEP)
    for _ in range(3):
        carry = (total.astype(F32) + th[0:1] * carry.astype(F32)).astype(BF16)
        carry = lax.ppermute(carry, "ctx", Z_STEP)
    backs = pl.pallas_call(
        back_kernel,
        in_specs=smem(1) + vmem(3),
        out_specs=vmem(4),
        out_shape=[quarter] * 4,
        compiler_params=PARAMS,
        name="row_states",
    )(place, prefix, pth, carry)
    incoming = [backs[0]] + [lax.ppermute(backs[k], "ctx", x_shift(k)) for k in (1, 2, 3)]

    y_local = pl.pallas_call(
        local_kernel,
        in_specs=smem(2) + vmem(6),
        out_specs=pl.BlockSpec(memory_space=pltpu.VMEM),
        out_shape=sds((toks, lanes), F32),
        compiler_params=PARAMS,
        name="within_chunk",
    )(place, rollout_lengths, mixer_input, input_map, output_map, dd, cumt, skip_gain[None, :])

    q_heads = queries.shape[1] // HEAD_DIM
    window = 17
    attended = pl.pallas_call(
        attend_kernel,
        in_specs=smem(2) + vmem(9),
        out_specs=pl.BlockSpec(memory_space=pltpu.VMEM),
        out_shape=sds((q_heads, toks, HEAD_DIM), BF16),
        scratch_shapes=[
            pltpu.VMEM((window, toks, 2 * HEAD_DIM), BF16),
            pltpu.VMEM((window, toks, 2 * HEAD_DIM), BF16),
            pltpu.VMEM((q_heads, toks, 2 * HEAD_DIM), BF16),
            pltpu.VMEM((window, toks, toks), F32),
            pltpu.VMEM((window, toks, toks), F32),
        ],
        compiler_params=PARAMS,
        name="attend",
    )(place, rollout_lengths, queries, *zs, *gs)

    cols = out_weight.shape[1] // (2 * NY)

    def column(i, place):
        y = lax.rem(place[2] + lax.rem(i, NY), NY)
        core = jnp.where(i < NY, 1 - place[3], place[3])
        return (0, 2 * y + core)

    partial = pl.pallas_call(
        project_kernel,
        grid_spec=pltpu.PrefetchScalarGridSpec(
            num_scalar_prefetch=1,
            grid=(2 * NY,),
            in_specs=[
                pl.BlockSpec((q_heads, toks, HEAD_DIM), lambda i, place: (0, 0, 0)),
                pl.BlockSpec((out_weight.shape[0], cols), column),
            ],
            out_specs=pl.BlockSpec((1, toks, cols), lambda i, place: (i, 0, 0)),
            scratch_shapes=[pltpu.VMEM((toks, q_heads * HEAD_DIM), BF16)],
        ),
        out_shape=sds((2 * NY, toks, cols), BF16),
        compiler_params=PARAMS,
        name="project",
    )(place, attended, out_weight)
    twin = lax.ppermute(partial[:NY], "tp", TWIN)
    summed = [partial[NY + k].astype(F32) + twin[k].astype(F32) for k in range(NY)]
    block_out = summed[0]
    for k in (1, 2, 3):
        block_out = block_out + lax.ppermute(summed[k].astype(BF16), "tp", y_shift(k)).astype(F32)
    block_out = block_out.astype(BF16)

    mamba_out = pl.pallas_call(
        gate_kernel,
        in_specs=smem(1) + vmem(9),
        out_specs=pl.BlockSpec(memory_space=pltpu.VMEM),
        out_shape=sds((toks, lanes), BF16),
        scratch_shapes=[pltpu.VMEM((NX, STATE, QUARTER), BF16)],
        compiler_params=PARAMS,
        name="carry_gate_norm",
    )(place, y_local, output_map, lead, gate_input, norm_gain[None, :], *incoming)
    return (mamba_out, block_out)


def solution(mesh):
    both = P("ctx", "tp")
    return jax.shard_map(
        body,
        mesh=mesh,
        in_specs=(both, both, both, both, P("tp", "ctx"), P("tp"), P("tp"), P("tp"), P("tp"),
                  both, both, both, P("tp", None), P()),
        out_specs=(both, both),
        check_vma=False,
    )
```

```python
import math

import jax
import jax.numpy as jnp
from jax import lax
from jax.experimental import pallas as pl
from jax.experimental.pallas import tpu as pltpu
from jax.sharding import PartitionSpec as P

HEAD_P = 64
STATE = 256
HEAD_DIM = 128
NZ = 8
NX = 4
NY = 4
LOG2E = math.log2(math.e)
EPS = 1e-05
BIG = -1e30
F32 = jnp.float32
BF16 = jnp.bfloat16
EXTRA = 16
QUARTER = 512


def iota(shape, dim):
    return lax.broadcasted_iota(jnp.int32, shape, dim)


def split3(a):
    hi = a.astype(BF16)
    rest = a - hi.astype(F32)
    mid = rest.astype(BF16)
    low = (rest - mid.astype(F32)).astype(BF16)
    return hi, mid, low


def spread(a, expand, terms=3):
    total = None
    for part in split3(a)[:terms]:
        one = jnp.dot(part, expand, preferred_element_type=F32)
        total = one if total is None else total + one
    return total


def expander(heads, lanes):
    return (iota((heads, lanes), 1) // HEAD_P == iota((heads, lanes), 0)).astype(F32).astype(BF16)


def place_of():
    ctx = lax.axis_index("ctx")
    return ctx // NX, lax.rem(ctx, NX)


def ends_of(lengths):
    e0 = lengths[0]
    e1 = e0 + lengths[1]
    e2 = e1 + lengths[2]
    return e0, e1, e2, e2 + lengths[3]


def rollout_at(pos, ends):
    count = jnp.zeros_like(pos)
    for e in ends:
        count = count + (pos >= e).astype(jnp.int32)
    return jnp.where(pos < 0, -1, count)


def pack_kernel(k_ref, v_ref, kv_ref):
    kv_ref[:, :HEAD_DIM] = k_ref[...]
    kv_ref[:, HEAD_DIM:] = v_ref[...]


def relay_kernel(a_ref, after, o_ref):
    o_ref[...] = a_ref[...]


def join_kernel(a_ref, b_ref, o_ref):
    rows = a_ref.shape[0]
    o_ref[:rows, :] = a_ref[...]
    o_ref[rows:, :] = b_ref[...]


def edge_kernel(own_ref, last_ref, b_ref, o1, o2, o3):
    xi = place_of()[1]
    rows = own_ref.shape[0]
    for k, out in ((1, o1), (2, o2), (3, o3)):
        out[rows:, :] = b_ref[...]

        @pl.when(xi + k < NX)
        def _():
            out[:rows, :] = own_ref[...]

        @pl.when(xi + k >= NX)
        def _():
            out[:rows, :] = last_ref[...]


def state_kernel(lengths, x_ref, b_ref, raw_ref, bias_ref, alog_ref,
                 o0, o1, o2, o3, d_ref, cumt_ref, lead_ref, scr):
    heads, toks = raw_ref.shape
    lanes = x_ref.shape[1]
    zi, xi = place_of()
    first = (zi * NX + xi) * toks
    ends = ends_of(lengths)
    width = jax.nn.softplus(raw_ref[...].T + bias_ref[...])
    rate2 = width * (-LOG2E * jnp.exp(alog_ref[...]))
    lower = (iota((toks, toks), 0) >= iota((toks, toks), 1)).astype(F32).astype(BF16)
    cumt = sum(jnp.dot(lower, part, preferred_element_type=F32) for part in split3(rate2))
    d_ref[...] = (cumt - jnp.log2(width)).T
    cumt_ref[...] = cumt
    before = rollout_at(first - 1, ends)
    last = rollout_at(first + (toks - 1), ends)
    roll = rollout_at(first + iota((toks, heads), 0), ends)
    lead_ref[...] = jnp.where(roll == before, jnp.exp2(cumt), 0.0)
    end = cumt[toks - 1:toks, :]
    tail = jnp.where(roll == last, jnp.exp2(end - cumt), 0.0) * width
    expand = expander(heads, lanes)
    xw = (spread(tail, expand, 2) * x_ref[...].astype(F32)).astype(BF16)
    state = lax.dot_general(b_ref[...], xw, (((0,), (0,)), ((), ())), preferred_element_type=F32)
    through = jnp.where(last == before, jnp.exp2(end), 0.0)
    th = [jnp.dot(part, expand, preferred_element_type=F32) for part in split3(through)]
    row = iota((EXTRA, lanes), 0)
    extra = jnp.where(row == 0, th[0], jnp.where(row == 1, th[1], jnp.where(row == 2, th[2], 0.0)))
    whole = jnp.concatenate([state, extra], axis=0).astype(BF16)
    for q in range(NX):
        scr[q] = whole[:, q * QUARTER:(q + 1) * QUARTER]
    for k, out in enumerate((o0, o1, o2, o3)):
        out[...] = scr[lax.rem(xi + k, NX)]


def with_decay(ref, state, decay):
    hi, mid, low = split3(decay)
    row = iota((EXTRA, QUARTER), 0)
    extra = jnp.where(row == 0, hi.astype(F32), jnp.where(row == 1, mid.astype(F32), jnp.where(row == 2, low.astype(F32), 0.0)))
    ref[:STATE, :] = state.astype(BF16)
    ref[STATE:, :] = extra.astype(BF16)


def decay_in(tail):
    tail = tail.astype(F32)
    return tail[0:1] + tail[1:2] + tail[2:3]


def row_kernel(a0, a1, a2, a3, after, p_ref, t_ref, pth_ref, scr):
    zi, xi = place_of()
    for k, a in enumerate((a0, a1, a2, a3)):
        scr[lax.rem(xi - k + NX, NX)] = a[...]
    total = jnp.zeros((STATE, QUARTER), F32)
    through = jnp.ones((1, QUARTER), F32)
    for j in range(NX):
        p_ref[j] = total.astype(BF16)
        pth_ref[j] = jnp.broadcast_to(through, (8, QUARTER))
        one = decay_in(scr[j, STATE:STATE + EXTRA, :])
        total = one * total + scr[j, :STATE, :].astype(F32)
        through = through * one
    with_decay(t_ref, total, jnp.where(zi > 0, through, 0.0))


def pair_kernel(t_ref, came_ref, o_ref):
    through = decay_in(t_ref[STATE:, :])
    total = t_ref[:STATE, :].astype(F32) + through * came_ref[:STATE, :].astype(F32)
    with_decay(o_ref, total, through * decay_in(came_ref[STATE:, :]))


def back_kernel(p_ref, pth_ref, near_ref, far_ref, o0, o1, o2, o3):
    zi, xi = place_of()
    came = near_ref[:STATE, :].astype(F32) + decay_in(near_ref[STATE:, :]) * far_ref[:STATE, :].astype(F32)
    came = jnp.where(zi > 0, came, 0.0)
    for k, out in enumerate((o0, o1, o2, o3)):
        j = lax.rem(xi + k, NX)
        out[...] = (p_ref[j].astype(F32) + pth_ref[j][0:1] * came).astype(BF16)


def local_kernel(lengths, x_ref, b_ref, c_ref, d_ref, cumt_ref, skip_ref, y_ref, token_ref):
    token_ref[...] = jnp.zeros_like(token_ref)
    toks, lanes = x_ref.shape
    heads = d_ref.shape[0]
    half = toks // 2
    zi, xi = place_of()
    first = (zi * NX + xi) * toks
    ends = ends_of(lengths)
    roll_t = rollout_at(first + iota((toks, toks), 0), ends)
    roll_s = rollout_at(first + iota((toks, toks), 1), ends)
    seen = (roll_t == roll_s) & (iota((toks, toks), 0) >= iota((toks, toks), 1))
    inner = lax.dot_general(c_ref[...], b_ref[...], (((1,), (1,)), ((), ())), preferred_element_type=F32)
    inner = jnp.where(seen, inner, 0.0)
    left = iota((half, 128), 1) < HEAD_P
    skip = spread(skip_ref[...], expander(heads, lanes))
    d_all = d_ref[...]
    cumt = cumt_ref[...]
    for pair in range(heads // 2):
        cols = slice(pair * 128, (pair + 1) * 128)
        x_pair = x_ref[:, cols]
        for rows, width in ((slice(0, half), half), (slice(half, toks), toks)):
            res = []
            for h in (2 * pair, 2 * pair + 1):
                diff = cumt[rows, h:h + 1] - d_all[h:h + 1, :width]
                mix = (jnp.exp2(jnp.minimum(diff, 64.0)) * inner[rows, :width]).astype(BF16)
                res.append(jnp.dot(mix, x_pair[:width], preferred_element_type=F32))
            y_ref[rows, cols] = jnp.where(left, res[0], res[1]) + skip[:, cols] * x_pair[rows].astype(F32)


def gate_kernel(y_ref, c_ref, lead_ref, gate_ref, gain_ref, i0, i1, i2, i3, out_ref, scr):
    toks, lanes = y_ref.shape
    heads = lead_ref.shape[1]
    xi = place_of()[1]
    for k, a in enumerate((i0, i1, i2, i3)):
        scr[lax.rem(xi - k + NX, NX)] = a[...]
    expand = expander(heads, lanes)
    square = jnp.zeros((toks, 1), F32)
    held = []
    for q in range(NX):
        cols = slice(q * QUARTER, (q + 1) * QUARTER)
        carried = jnp.dot(c_ref[...], scr[q], preferred_element_type=F32)
        lead = spread(lead_ref[...], expand[:, cols], 2)
        v = gate_ref[:, cols].astype(F32)
        gated = (y_ref[:, cols] + lead * carried) * (v / (1.0 + jnp.exp(-v)))
        square = square + jnp.sum(gated * gated, axis=1, keepdims=True)
        held.append(gated)
    factor = lax.rsqrt(square * (1.0 / lanes) + EPS)
    for q in range(NX):
        cols = slice(q * QUARTER, (q + 1) * QUARTER)
        out_ref[:, cols] = (held[q] * factor * gain_ref[:, cols]).astype(BF16)


def fill(lengths, first, slots, k_buf, v_buf):
    toks = k_buf.shape[1]
    lane = iota((toks, HEAD_DIM), 1)
    row = iota((toks, HEAD_DIM), 0)
    ones = (lane == 0).astype(F32).astype(BF16)
    ends = ends_of(lengths)
    begins = (0,) + ends[:3]
    lane_row = iota((1, HEAD_DIM), 1)
    low = jnp.zeros((1, HEAD_DIM), jnp.int32)
    high = low
    for r in range(4):
        low = jnp.where(lane_row == r, begins[r], low)
        high = jnp.where(lane_row == r, ends[r], high)
    for i, (slot, kv) in enumerate(slots):
        start = first + (slot - 16) * toks
        k_buf[i, :, :HEAD_DIM] = kv[:, :HEAD_DIM]
        v_buf[i, :, :HEAD_DIM] = kv[:, HEAD_DIM:]
        k_buf[i, :, HEAD_DIM:] = jnp.where((row >= low - start) & (row < high - start), 0.0, BIG).astype(BF16)
        v_buf[i, :, HEAD_DIM:] = ones


def fill_queries(ends, first, q_ref, q_buf):
    heads, toks = q_buf.shape[:2]
    lane = iota((toks, HEAD_DIM), 1)
    mine = (rollout_at(first + iota((toks, 1), 0), ends) == lane).astype(F32).astype(BF16)
    for h in range(heads):
        q_buf[h, :, :HEAD_DIM] = q_ref[:, h * HEAD_DIM:(h + 1) * HEAD_DIM]
        q_buf[h, :, HEAD_DIM:] = mine


def over_heads(heads, chunks, q_buf, k_buf, v_buf, s_a, s_b, causal_at, start, finish):
    toks = q_buf.shape[1]
    scale = LOG2E / math.sqrt(HEAD_DIM)
    causal = iota((toks, toks), 0) >= iota((toks, toks), 1)

    def scores(h, buf, j, peak):
        s = lax.dot_general(q_buf[h], k_buf[j], (((1,), (1,)), ((), ())), preferred_element_type=F32)
        if j == causal_at:
            s = jnp.where(causal, s, BIG)
        buf[j] = s
        return jnp.maximum(peak, jnp.maximum(s[:, :128], s[:, 128:]))

    def both(h, buf_now, buf_next, peak):
        top = jnp.max(peak, axis=1, keepdims=True)
        acc = start[1](h, top, scale)
        nxt = jnp.minimum(h + 1, heads - 1)
        peak = start[0](nxt)
        for j in range(chunks):
            peak = scores(nxt, buf_next, j, peak)
            p = jnp.exp2((buf_now[j] - top) * scale).astype(BF16)
            acc = acc + jnp.dot(p, v_buf[j], preferred_element_type=F32)
        finish(h, top, acc)
        return peak

    def two(i, peak):
        peak = both(2 * i, s_a, s_b, peak)
        return both(2 * i + 1, s_b, s_a, peak)

    peak = start[0](0)
    for j in range(chunks):
        peak = scores(0, s_a, j, peak)
    lax.fori_loop(0, heads // 2, two, peak)


def attend_first_kernel(lengths, q_ref, own, z1, z2, z3, g1, g2, g3, after, acc_ref, ml_ref,
                        k_buf, v_buf, q_buf, s_a, s_b):
    heads, toks = q_buf.shape[:2]
    zi, xi = place_of()
    first = (zi * NX + xi) * toks
    ends = ends_of(lengths)
    slots = [(16, own), (12, z1), (8, z2), (4, z3)]
    for k, g in ((1, g1), (2, g2), (3, g3)):
        ahead = xi >= k
        slots.append((jnp.where(ahead, 12 - k, 16 - k), g[0:toks, :]))
        slots.append((jnp.where(ahead, 8 - k, 12 - k), g[toks:2 * toks, :]))
    fill(lengths, first, slots, k_buf, v_buf)
    fill_queries(ends, first, q_ref, q_buf)
    lane = iota((toks, HEAD_DIM), 1)

    def finish(h, top, acc):
        acc_ref[h] = acc[:, :HEAD_DIM]
        ml_ref[h] = jnp.where(lane == 0, acc[:, HEAD_DIM:], top)

    start = (lambda h: jnp.full((toks, HEAD_DIM), BIG, F32),
             lambda h, top, scale: jnp.zeros((toks, 2 * HEAD_DIM), F32))
    over_heads(heads, len(slots), q_buf, k_buf, v_buf, s_a, s_b, 0, start, finish)


def attend_second_kernel(lengths, q_ref, z4, g1, g2, g3, acc_ref, ml_ref, after, out_ref,
                         k_buf, v_buf, q_buf, s_a, s_b):
    heads, toks = q_buf.shape[:2]
    zi, xi = place_of()
    first = (zi * NX + xi) * toks
    ends = ends_of(lengths)
    slots = [(0, z4)]
    for k, g in ((1, g1), (2, g2), (3, g3)):
        ahead = xi >= k
        slots.append((jnp.where(ahead, 16 - k, 4 - k), g[0:toks, :]))
        slots.append((jnp.where(ahead, 4 - k, 8 - k), g[toks:2 * toks, :]))
    fill(lengths, first, slots, k_buf, v_buf)
    fill_queries(ends, first, q_ref, q_buf)
    lane = iota((toks, HEAD_DIM), 1)

    def begin(h, top, scale):
        ml = ml_ref[h]
        old = jnp.exp2((ml[:, 1:2] - top) * scale)
        total = jnp.where(lane == 0, ml, 0.0)
        return jnp.concatenate([acc_ref[h], total], axis=1) * old

    def finish(h, top, acc):
        res = acc[:, :HEAD_DIM] / acc[:, HEAD_DIM:HEAD_DIM + 1]
        out_ref[h] = res.astype(BF16)

    start = (lambda h: jnp.where(lane == 0, BIG, ml_ref[h]), begin)
    over_heads(heads, len(slots), q_buf, k_buf, v_buf, s_a, s_b, None, start, finish)


def project_kernel(a_ref, w_ref, after, send_ref, keep_ref, wide, both):
    h = a_ref.shape[0]
    cols = both.shape[2]
    tp = lax.axis_index("tp")
    y, core = tp // 2, lax.rem(tp, 2)
    for i in range(h):
        wide[:, i * HEAD_DIM:(i + 1) * HEAD_DIM] = a_ref[i]
    for k in range(NY):
        at = pl.multiple_of(lax.rem(y + k, NY) * (2 * cols), 2 * cols)
        for c in range(2):
            both[c] = jnp.dot(wide[...], w_ref[:, pl.ds(at + c * cols, cols)], preferred_element_type=F32).astype(BF16)
        send_ref[k] = both[1 - core]
        keep_ref[k] = both[core]


def vmem(n):
    return [pl.BlockSpec(memory_space=pltpu.VMEM)] * n


def smem(n):
    return [pl.BlockSpec(memory_space=pltpu.SMEM)] * n


def cost(us):
    return pl.CostEstimate(flops=int(us * 1.1e9), transcendentals=0, bytes_accessed=int(us * 3.2e6))


def kept(shape, dtype):
    return pltpu.VMEM(shape, dtype)


def sds(shape, dtype):
    return jax.ShapeDtypeStruct(shape, dtype)


def far(a):
    return pltpu.with_memory_space_constraint(a, pltpu.HBM)


def params(mib):
    return pltpu.CompilerParams(vmem_limit_bytes=mib * 1024 * 1024)


def near(a):
    return pltpu.with_memory_space_constraint(a, pltpu.VMEM)


def x_shift(k):
    return [(NX * z + x, NX * z + (x + k) % NX) for z in range(NZ) for x in range(NX)]


def y_shift(k):
    return [(2 * y + c, 2 * ((y + k) % NY) + c) for y in range(NY) for c in range(2)]


def z_shift(k):
    return [(NX * z + x, NX * ((z + k) % NZ) + x) for z in range(NZ) for x in range(NX)]


TWIN = [(i, i ^ 1) for i in range(2 * NY)]


def body(mixer_input, gate_input, input_map, output_map, step_raw, step_bias, decay_log, skip_gain,
         norm_gain, queries, key_heads, value_heads, out_weight, rollout_lengths):
    toks, lanes = mixer_input.shape
    heads = step_raw.shape[0]
    msg = kept((STATE + EXTRA, QUARTER), BF16)
    quarter = kept((STATE, QUARTER), BF16)

    anywhere = [pl.BlockSpec(memory_space=pl.ANY)]
    chunk = kept((toks, 2 * HEAD_DIM), BF16)
    chunks = kept((2 * toks, 2 * HEAD_DIM), BF16)
    one = pl.BlockSpec(memory_space=pltpu.VMEM)
    own = pl.pallas_call(
        pack_kernel, in_specs=vmem(2), out_specs=one, out_shape=chunk,
        compiler_params=params(4), cost_estimate=cost(0.5), name="pack",
    )(far(key_heads), far(value_heads))
    zs = [own, lax.ppermute(own, "ctx", z_shift(1))]
    o0, o1, o2, o3, dd, cumt, lead = pl.pallas_call(
        state_kernel,
        in_specs=smem(1) + vmem(5),
        out_specs=vmem(7),
        out_shape=[msg] * 4 + [kept((heads, toks), F32), kept((toks, heads), F32), kept((toks, heads), F32)],
        scratch_shapes=[pltpu.VMEM((NX, STATE + EXTRA, QUARTER), BF16)],
        compiler_params=params(16),
        cost_estimate=cost(3),
        name="chunk_states",
    )(*map(far, (rollout_lengths, mixer_input, input_map, step_raw, step_bias[None, :], decay_log[None, :])))
    came = [o0] + [lax.ppermute(o, "ctx", x_shift(k)) for k, o in ((1, o1), (2, o2), (3, o3))]

    y_local, token = pl.pallas_call(
        local_kernel,
        in_specs=smem(1) + vmem(6),
        out_specs=vmem(2),
        out_shape=[kept((toks, lanes), F32), kept((8, 128), F32)],
        compiler_params=params(16),
        cost_estimate=cost(2.5),
        name="within_chunk",
    )(rollout_lengths, near(mixer_input), near(input_map), near(output_map), *map(near, (dd, cumt)), skip_gain[None, :])

    sent = pl.pallas_call(
        relay_kernel, in_specs=vmem(1) + anywhere, out_specs=one, out_shape=chunk,
        compiler_params=params(4), cost_estimate=cost(0.5), name="relay",
    )(near(zs[1]), token)
    for _ in range(3):
        sent = lax.ppermute(sent, "ctx", z_shift(1))
        zs.append(sent)
    soon = pl.pallas_call(
        join_kernel, in_specs=vmem(2), out_specs=one, out_shape=chunks,
        compiler_params=params(4), cost_estimate=cost(0.5), name="two_chunks",
    )(near(zs[1]), near(zs[2]))
    gs = [lax.ppermute(soon, "ctx", x_shift(k)) for k in (1, 2, 3)]
    later = pl.pallas_call(
        edge_kernel, in_specs=vmem(3), out_specs=vmem(3), out_shape=[chunks] * 3,
        compiler_params=params(6), cost_estimate=cost(0.5), name="edge_chunks",
    )(near(own), near(zs[4]), near(zs[3]))
    gs = gs + [lax.ppermute(a, "ctx", x_shift(k)) for k, a in zip((1, 2, 3), later)]

    prefix, total, pth = pl.pallas_call(
        row_kernel,
        in_specs=vmem(4) + [pl.BlockSpec(memory_space=pl.ANY)],
        out_specs=vmem(3),
        out_shape=[kept((NX, STATE, QUARTER), BF16), msg, kept((NX, 8, QUARTER), F32)],
        scratch_shapes=[pltpu.VMEM((NX, STATE + EXTRA, QUARTER), BF16)],
        compiler_params=params(12),
        cost_estimate=cost(1),
        name="row_scan",
    )(*map(near, came), token)

    once = lax.ppermute(total, "ctx", z_shift(1))
    pair = pl.pallas_call(
        pair_kernel,
        in_specs=vmem(2),
        out_specs=pl.BlockSpec(memory_space=pltpu.VMEM),
        out_shape=msg,
        compiler_params=params(8),
        cost_estimate=cost(0.5),
        name="two_rows",
    )(near(total), near(once))
    twice = lax.ppermute(pair, "ctx", z_shift(1))
    before = lax.ppermute(twice, "ctx", z_shift(2))
    backs = pl.pallas_call(
        back_kernel,
        in_specs=vmem(4),
        out_specs=vmem(4),
        out_shape=[quarter] * 4,
        compiler_params=params(8),
        cost_estimate=cost(1),
        name="row_states",
    )(*map(near, (prefix, pth, twice, before)))
    incoming = [backs[0]] + [lax.ppermute(backs[k], "ctx", x_shift(k)) for k in (1, 2, 3)]

    q_heads = queries.shape[1] // HEAD_DIM
    def scratch(chunks):
        wide = pltpu.VMEM((chunks, toks, 2 * HEAD_DIM), BF16)
        logits = pltpu.VMEM((chunks, toks, toks), F32)
        return [wide, wide, pltpu.VMEM((q_heads, toks, 2 * HEAD_DIM), BF16), logits, logits]

    acc, ml = pl.pallas_call(
        attend_first_kernel,
        in_specs=smem(1) + vmem(8) + anywhere,
        out_specs=vmem(2),
        out_shape=[kept((q_heads, toks, HEAD_DIM), F32)] * 2,
        scratch_shapes=scratch(10),
        compiler_params=params(24),
        cost_estimate=cost(10),
        name="attend_first",
    )(rollout_lengths, queries, *map(near, (*zs[:4], *gs[:3])), pair)
    attended = pl.pallas_call(
        attend_second_kernel,
        in_specs=smem(1) + vmem(7) + anywhere,
        out_specs=pl.BlockSpec(memory_space=pltpu.VMEM),
        out_shape=kept((q_heads, toks, HEAD_DIM), BF16),
        scratch_shapes=scratch(7),
        compiler_params=params(20),
        cost_estimate=cost(8),
        name="attend_second",
    )(rollout_lengths, queries, *map(near, (zs[4], *gs[3:], acc, ml)), twice)

    cols = out_weight.shape[1] // (2 * NY)
    send, keep = pl.pallas_call(
        project_kernel,
        in_specs=vmem(2) + anywhere,
        out_specs=vmem(2),
        out_shape=[kept((NY, toks, cols), BF16)] * 2,
        scratch_shapes=[pltpu.VMEM((toks, q_heads * HEAD_DIM), BF16), pltpu.VMEM((2, toks, cols), BF16)],
        compiler_params=params(16),
        cost_estimate=cost(3),
        name="project",
    )(near(attended), near(out_weight), before)
    twin = lax.ppermute(send, "tp", TWIN)
    summed = [keep[k].astype(F32) + twin[k].astype(F32) for k in range(NY)]
    block_out = summed[0]
    for k in (1, 2, 3):
        block_out = block_out + lax.ppermute(summed[k].astype(BF16), "tp", y_shift(k)).astype(F32)
    block_out = block_out.astype(BF16)

    mamba_out = pl.pallas_call(
        gate_kernel,
        in_specs=vmem(9),
        out_specs=pl.BlockSpec(memory_space=pltpu.VMEM),
        out_shape=sds((toks, lanes), BF16),
        scratch_shapes=[pltpu.VMEM((NX, STATE, QUARTER), BF16)],
        compiler_params=params(16),
        cost_estimate=cost(2.5),
        name="carry_gate_norm",
    )(*map(near, (y_local, output_map, lead, gate_input)), norm_gain[None, :], *map(near, incoming))
    return (mamba_out, block_out)


def solution(mesh):
    both = P("ctx", "tp")
    return jax.shard_map(
        body,
        mesh=mesh,
        in_specs=(both, both, both, both, P("tp", "ctx"), P("tp"), P("tp"), P("tp"), P("tp"),
                  both, both, both, P("tp", None), P()),
        out_specs=(both, both),
        check_vma=False,
    )
```

```python
import math

import jax
import jax.numpy as jnp
from jax import lax
from jax.experimental import pallas as pl
from jax.experimental.pallas import tpu as pltpu
from jax.sharding import PartitionSpec as P

HEAD_P = 64
STATE = 256
HEAD_DIM = 128
NZ = 8
NX = 4
NY = 4
LOG2E = math.log2(math.e)
EPS = 1e-05
BIG = -1e30
F32 = jnp.float32
BF16 = jnp.bfloat16
EXTRA = 16
QUARTER = 512


def iota(shape, dim):
    return lax.broadcasted_iota(jnp.int32, shape, dim)


def split3(a):
    hi = a.astype(BF16)
    rest = a - hi.astype(F32)
    mid = rest.astype(BF16)
    low = (rest - mid.astype(F32)).astype(BF16)
    return hi, mid, low


def spread(a, expand, terms=3):
    total = None
    for part in split3(a)[:terms]:
        one = jnp.dot(part, expand, preferred_element_type=F32)
        total = one if total is None else total + one
    return total


def expander(heads, lanes):
    return (iota((heads, lanes), 1) // HEAD_P == iota((heads, lanes), 0)).astype(F32).astype(BF16)


def place_of():
    ctx = lax.axis_index("ctx")
    return ctx // NX, lax.rem(ctx, NX)


def ends_of(lengths):
    e0 = lengths[0]
    e1 = e0 + lengths[1]
    e2 = e1 + lengths[2]
    return e0, e1, e2, e2 + lengths[3]


def rollout_at(pos, ends):
    count = jnp.zeros_like(pos)
    for e in ends:
        count = count + (pos >= e).astype(jnp.int32)
    return jnp.where(pos < 0, -1, count)


def pack_kernel(k_ref, v_ref, kv_ref):
    kv_ref[:, :HEAD_DIM] = k_ref[...]
    kv_ref[:, HEAD_DIM:] = v_ref[...]


def relay_kernel(a_ref, after, o_ref):
    o_ref[...] = a_ref[...]


def join_kernel(a_ref, b_ref, o_ref):
    rows = a_ref.shape[0]
    o_ref[:rows, :] = a_ref[...]
    o_ref[rows:, :] = b_ref[...]


def edge_kernel(own_ref, last_ref, b_ref, after, o1, o2, o3):
    xi = place_of()[1]
    rows = own_ref.shape[0]
    for k, out in ((1, o1), (2, o2), (3, o3)):
        out[rows:, :] = b_ref[...]

        @pl.when(xi + k < NX)
        def _():
            out[:rows, :] = own_ref[...]

        @pl.when(xi + k >= NX)
        def _():
            out[:rows, :] = last_ref[...]


def state_kernel(lengths, x_ref, b_ref, raw_ref, bias_ref, alog_ref, k_ref, v_ref,
                 o0, o1, o2, o3, kv_ref, d_ref, cumt_ref, lead_ref, scr):
    heads, toks = raw_ref.shape
    lanes = x_ref.shape[1]
    zi, xi = place_of()
    first = (zi * NX + xi) * toks
    ends = ends_of(lengths)
    kv_ref[:, :HEAD_DIM] = k_ref[...]
    kv_ref[:, HEAD_DIM:] = v_ref[...]
    width = jax.nn.softplus(raw_ref[...].T + bias_ref[...])
    rate2 = width * (-LOG2E * jnp.exp(alog_ref[...]))
    lower = (iota((toks, toks), 0) >= iota((toks, toks), 1)).astype(F32).astype(BF16)
    cumt = sum(jnp.dot(lower, part, preferred_element_type=F32) for part in split3(rate2))
    d_ref[...] = (cumt - jnp.log2(width)).T
    cumt_ref[...] = cumt
    before = rollout_at(first - 1, ends)
    last = rollout_at(first + (toks - 1), ends)
    roll = rollout_at(first + iota((toks, heads), 0), ends)
    lead_ref[...] = jnp.where(roll == before, jnp.exp2(cumt), 0.0)
    end = cumt[toks - 1:toks, :]
    tail = jnp.where(roll == last, jnp.exp2(end - cumt), 0.0) * width
    expand = expander(heads, lanes)
    xw = (spread(tail, expand, 2) * x_ref[...].astype(F32)).astype(BF16)
    state = lax.dot_general(b_ref[...], xw, (((0,), (0,)), ((), ())), preferred_element_type=F32)
    through = jnp.where(last == before, jnp.exp2(end), 0.0)
    th = [jnp.dot(part, expand, preferred_element_type=F32) for part in split3(through)]
    row = iota((EXTRA, lanes), 0)
    extra = jnp.where(row == 0, th[0], jnp.where(row == 1, th[1], jnp.where(row == 2, th[2], 0.0)))
    whole = jnp.concatenate([state, extra], axis=0).astype(BF16)
    for q in range(NX):
        scr[q] = whole[:, q * QUARTER:(q + 1) * QUARTER]
    for k, out in enumerate((o0, o1, o2, o3)):
        out[...] = scr[lax.rem(xi + k, NX)]


def with_decay(ref, state, decay):
    hi, mid, low = split3(decay)
    row = iota((EXTRA, QUARTER), 0)
    extra = jnp.where(row == 0, hi.astype(F32), jnp.where(row == 1, mid.astype(F32), jnp.where(row == 2, low.astype(F32), 0.0)))
    ref[:STATE, :] = state.astype(BF16)
    ref[STATE:, :] = extra.astype(BF16)


def decay_in(tail):
    tail = tail.astype(F32)
    return tail[0:1] + tail[1:2] + tail[2:3]


def row_kernel(a0, a1, a2, a3, after, p_ref, t_ref, pth_ref, scr):
    zi, xi = place_of()
    for k, a in enumerate((a0, a1, a2, a3)):
        scr[lax.rem(xi - k + NX, NX)] = a[...]
    total = jnp.zeros((STATE, QUARTER), F32)
    through = jnp.ones((1, QUARTER), F32)
    for j in range(NX):
        p_ref[j] = total.astype(BF16)
        pth_ref[j] = jnp.broadcast_to(through, (8, QUARTER))
        one = decay_in(scr[j, STATE:STATE + EXTRA, :])
        total = one * total + scr[j, :STATE, :].astype(F32)
        through = through * one
    with_decay(t_ref, total, jnp.where(zi > 0, through, 0.0))


def pair_kernel(t_ref, came_ref, o_ref):
    through = decay_in(t_ref[STATE:, :])
    total = t_ref[:STATE, :].astype(F32) + through * came_ref[:STATE, :].astype(F32)
    with_decay(o_ref, total, through * decay_in(came_ref[STATE:, :]))


def back_kernel(p_ref, pth_ref, near_ref, far_ref, o0, o1, o2, o3):
    zi, xi = place_of()
    came = near_ref[:STATE, :].astype(F32) + decay_in(near_ref[STATE:, :]) * far_ref[:STATE, :].astype(F32)
    came = jnp.where(zi > 0, came, 0.0)
    for k, out in enumerate((o0, o1, o2, o3)):
        j = lax.rem(xi + k, NX)
        out[...] = (p_ref[j].astype(F32) + pth_ref[j][0:1] * came).astype(BF16)


def local_kernel(lengths, x_ref, b_ref, c_ref, d_ref, cumt_ref, skip_ref, y_ref, token_ref):
    token_ref[...] = jnp.zeros_like(token_ref)
    toks, lanes = x_ref.shape
    heads = d_ref.shape[0]
    half = toks // 2
    zi, xi = place_of()
    first = (zi * NX + xi) * toks
    ends = ends_of(lengths)
    roll_t = rollout_at(first + iota((toks, toks), 0), ends)
    roll_s = rollout_at(first + iota((toks, toks), 1), ends)
    seen = (roll_t == roll_s) & (iota((toks, toks), 0) >= iota((toks, toks), 1))
    inner = lax.dot_general(c_ref[...], b_ref[...], (((1,), (1,)), ((), ())), preferred_element_type=F32)
    inner = jnp.where(seen, inner, 0.0)
    left = iota((half, 128), 1) < HEAD_P
    skip = spread(skip_ref[...], expander(heads, lanes))
    d_all = d_ref[...]
    cumt = cumt_ref[...]
    for pair in range(heads // 2):
        cols = slice(pair * 128, (pair + 1) * 128)
        x_pair = x_ref[:, cols]
        for rows, width in ((slice(0, half), half), (slice(half, toks), toks)):
            res = []
            for h in (2 * pair, 2 * pair + 1):
                diff = cumt[rows, h:h + 1] - d_all[h:h + 1, :width]
                mix = (jnp.exp2(jnp.minimum(diff, 64.0)) * inner[rows, :width]).astype(BF16)
                res.append(jnp.dot(mix, x_pair[:width], preferred_element_type=F32))
            y_ref[rows, cols] = jnp.where(left, res[0], res[1]) + skip[:, cols] * x_pair[rows].astype(F32)


def gate_kernel(y_ref, c_ref, lead_ref, gate_ref, gain_ref, i0, i1, i2, i3, out_ref, scr):
    toks, lanes = y_ref.shape
    heads = lead_ref.shape[1]
    xi = place_of()[1]
    for k, a in enumerate((i0, i1, i2, i3)):
        scr[lax.rem(xi - k + NX, NX)] = a[...]
    expand = expander(heads, lanes)
    square = jnp.zeros((toks, 1), F32)
    held = []
    for q in range(NX):
        cols = slice(q * QUARTER, (q + 1) * QUARTER)
        carried = jnp.dot(c_ref[...], scr[q], preferred_element_type=F32)
        lead = spread(lead_ref[...], expand[:, cols], 2)
        v = gate_ref[:, cols].astype(F32)
        gated = (y_ref[:, cols] + lead * carried) * (v / (1.0 + jnp.exp(-v)))
        square = square + jnp.sum(gated * gated, axis=1, keepdims=True)
        held.append(gated)
    factor = lax.rsqrt(square * (1.0 / lanes) + EPS)
    for q in range(NX):
        cols = slice(q * QUARTER, (q + 1) * QUARTER)
        out_ref[:, cols] = (held[q] * factor * gain_ref[:, cols]).astype(BF16)


def fill(lengths, first, slots, k_buf, v_buf):
    toks = k_buf.shape[1]
    lane = iota((toks, HEAD_DIM), 1)
    row = iota((toks, HEAD_DIM), 0)
    ones = (lane == 0).astype(F32).astype(BF16)
    ends = ends_of(lengths)
    begins = (0,) + ends[:3]
    lane_row = iota((1, HEAD_DIM), 1)
    low = jnp.zeros((1, HEAD_DIM), jnp.int32)
    high = low
    for r in range(4):
        low = jnp.where(lane_row == r, begins[r], low)
        high = jnp.where(lane_row == r, ends[r], high)
    for i, (slot, kv) in enumerate(slots):
        start = first + (slot - 16) * toks
        k_buf[i, :, :HEAD_DIM] = kv[:, :HEAD_DIM]
        v_buf[i, :, :HEAD_DIM] = kv[:, HEAD_DIM:]
        k_buf[i, :, HEAD_DIM:] = jnp.where((row >= low - start) & (row < high - start), 0.0, BIG).astype(BF16)
        v_buf[i, :, HEAD_DIM:] = ones


def fill_queries(ends, first, q_ref, q_buf):
    toks = q_ref.shape[0]
    lane = iota((toks, HEAD_DIM), 1)
    mine = (rollout_at(first + iota((toks, 1), 0), ends) == lane).astype(F32).astype(BF16)
    for h in range(q_ref.shape[1] // HEAD_DIM):
        rows = slice(h % 2 * toks, (h % 2 + 1) * toks)
        q_buf[h // 2, rows, :HEAD_DIM] = q_ref[:, h * HEAD_DIM:(h + 1) * HEAD_DIM]
        q_buf[h // 2, rows, HEAD_DIM:] = mine


def over_heads(heads, chunks, q_buf, k_buf, v_buf, s_a, s_b, causal_at, start, finish):
    rows, toks = q_buf.shape[1], k_buf.shape[1]
    scale = LOG2E / math.sqrt(HEAD_DIM)
    causal = iota((rows, toks), 0) % toks >= iota((rows, toks), 1)

    def scores(h, buf, j, peak):
        s = lax.dot_general(q_buf[h], k_buf[j], (((1,), (1,)), ((), ())), preferred_element_type=F32)
        if j == causal_at:
            s = jnp.where(causal, s, BIG)
        buf[j] = s
        return jnp.maximum(peak, jnp.maximum(s[:, :128], s[:, 128:]))

    def both(h, buf_now, buf_next, peak, more=True):
        top = jnp.max(peak, axis=1, keepdims=True)
        acc = start[1](h, top, scale)
        if more:
            peak = start[0](h + 1)
        for j in range(chunks):
            if more:
                peak = scores(h + 1, buf_next, j, peak)
            p = jnp.exp2((buf_now[j] - top) * scale).astype(BF16)
            acc = acc + jnp.dot(p, v_buf[j], preferred_element_type=F32)
        finish(h, top, acc)
        return peak

    def two(i, peak):
        peak = both(2 * i, s_a, s_b, peak)
        return both(2 * i + 1, s_b, s_a, peak)

    peak = start[0](0)
    for j in range(chunks):
        peak = scores(0, s_a, j, peak)
    peak = lax.fori_loop(0, heads // 2 - 1, two, peak)
    peak = both(heads - 2, s_a, s_b, peak)
    both(heads - 1, s_b, s_a, peak, False)


def two_of(ref, h):
    return jnp.concatenate([ref[2 * h], ref[2 * h + 1]], axis=0)


def attend_scratch(chunks, toks, heads):
    wide = pltpu.VMEM((chunks, toks, 2 * HEAD_DIM), BF16)
    logits = pltpu.VMEM((chunks, 2 * toks, toks), F32)
    return [wide, wide, pltpu.VMEM((heads // 2, 2 * toks, 2 * HEAD_DIM), BF16), logits, logits]


def attend_first_kernel(lengths, q_ref, own, z1, z2, z3, z4, g1, g2, g3, after, acc_ref, ml_ref,
                        k_buf, v_buf, q_buf, s_a, s_b):
    pairs, rows = q_buf.shape[:2]
    toks = q_ref.shape[0]
    zi, xi = place_of()
    first = (zi * NX + xi) * toks
    ends = ends_of(lengths)
    slots = [(16, own), (12, z1), (8, z2), (4, z3), (0, z4)]
    for k, g in ((1, g1), (2, g2), (3, g3)):
        ahead = xi >= k
        slots.append((jnp.where(ahead, 12 - k, 16 - k), g[0:toks, :]))
        slots.append((jnp.where(ahead, 8 - k, 12 - k), g[toks:2 * toks, :]))
    fill(lengths, first, slots, k_buf, v_buf)
    fill_queries(ends, first, q_ref, q_buf)
    lane = iota((rows, HEAD_DIM), 1)

    def finish(h, top, acc):
        ml = jnp.where(lane == 0, acc[:, HEAD_DIM:], top)
        for i in range(2):
            acc_ref[2 * h + i] = acc[i * toks:(i + 1) * toks, :HEAD_DIM]
            ml_ref[2 * h + i] = ml[i * toks:(i + 1) * toks]

    start = (lambda h: jnp.full((rows, HEAD_DIM), BIG, F32),
             lambda h, top, scale: jnp.zeros((rows, 2 * HEAD_DIM), F32))
    over_heads(pairs, len(slots), q_buf, k_buf, v_buf, s_a, s_b, 0, start, finish)


def attend_second_kernel(lengths, q_ref, g1, g2, g3, acc_ref, ml_ref, after, out_ref,
                         k_buf, v_buf, q_buf, s_a, s_b):
    pairs, rows = q_buf.shape[:2]
    toks = q_ref.shape[0]
    zi, xi = place_of()
    first = (zi * NX + xi) * toks
    ends = ends_of(lengths)
    slots = []
    for k, g in ((1, g1), (2, g2), (3, g3)):
        ahead = xi >= k
        slots.append((jnp.where(ahead, 16 - k, 4 - k), g[0:toks, :]))
        slots.append((jnp.where(ahead, 4 - k, 8 - k), g[toks:2 * toks, :]))
    fill(lengths, first, slots, k_buf, v_buf)
    fill_queries(ends, first, q_ref, q_buf)
    lane = iota((rows, HEAD_DIM), 1)

    def begin(h, top, scale):
        ml = two_of(ml_ref, h)
        old = jnp.exp2((ml[:, 1:2] - top) * scale)
        total = jnp.where(lane == 0, ml, 0.0)
        return jnp.concatenate([two_of(acc_ref, h), total], axis=1) * old

    def finish(h, top, acc):
        res = acc[:, :HEAD_DIM] / acc[:, HEAD_DIM:HEAD_DIM + 1]
        for i in range(2):
            out_ref[2 * h + i] = res[i * toks:(i + 1) * toks].astype(BF16)

    start = (lambda h: jnp.where(lane == 0, BIG, two_of(ml_ref, h)), begin)
    over_heads(pairs, len(slots), q_buf, k_buf, v_buf, s_a, s_b, None, start, finish)


def project_kernel(a_ref, w_ref, after, send_ref, keep_ref, wide, both):
    h = a_ref.shape[0]
    cols = both.shape[2]
    tp = lax.axis_index("tp")
    y, core = tp // 2, lax.rem(tp, 2)
    for i in range(h):
        wide[:, i * HEAD_DIM:(i + 1) * HEAD_DIM] = a_ref[i]
    for k in range(NY):
        at = pl.multiple_of(lax.rem(y + k, NY) * (2 * cols), 2 * cols)
        for c in range(2):
            both[c] = jnp.dot(wide[...], w_ref[:, pl.ds(at + c * cols, cols)], preferred_element_type=F32).astype(BF16)
        send_ref[k] = both[1 - core]
        keep_ref[k] = both[core]


def add_kernel(keep_ref, twin_ref, first_ref, *out_refs):
    first_ref[...] = keep_ref[0].astype(F32) + twin_ref[0].astype(F32)
    for k, out in enumerate(out_refs):
        out[...] = (keep_ref[k + 1].astype(F32) + twin_ref[k + 1].astype(F32)).astype(BF16)


def total_kernel(first_ref, a_ref, b_ref, c_ref, out_ref):
    total = first_ref[...] + a_ref[...].astype(F32)
    out_ref[...] = (total + b_ref[...].astype(F32) + c_ref[...].astype(F32)).astype(BF16)


def vmem(n):
    return [pl.BlockSpec(memory_space=pltpu.VMEM)] * n


def smem(n):
    return [pl.BlockSpec(memory_space=pltpu.SMEM)] * n


def cost(us):
    return pl.CostEstimate(flops=int(us * 1.1e9), transcendentals=0, bytes_accessed=int(us * 3.2e6))


def kept(shape, dtype):
    return pltpu.VMEM(shape, dtype)


def sds(shape, dtype):
    return jax.ShapeDtypeStruct(shape, dtype)


def far(a):
    return pltpu.with_memory_space_constraint(a, pltpu.HBM)


def params(mib):
    return pltpu.CompilerParams(vmem_limit_bytes=mib * 1024 * 1024)


def near(a):
    return pltpu.with_memory_space_constraint(a, pltpu.VMEM)


def x_shift(k):
    return [(NX * z + x, NX * z + (x + k) % NX) for z in range(NZ) for x in range(NX)]


def y_shift(k):
    return [(2 * y + c, 2 * ((y + k) % NY) + c) for y in range(NY) for c in range(2)]


def z_shift(k):
    return [(NX * z + x, NX * ((z + k) % NZ) + x) for z in range(NZ) for x in range(NX)]


TWIN = [(i, i ^ 1) for i in range(2 * NY)]


def body(mixer_input, gate_input, input_map, output_map, step_raw, step_bias, decay_log, skip_gain,
         norm_gain, queries, key_heads, value_heads, out_weight, rollout_lengths):
    toks, lanes = mixer_input.shape
    heads = step_raw.shape[0]
    msg = kept((STATE + EXTRA, QUARTER), BF16)
    quarter = kept((STATE, QUARTER), BF16)

    anywhere = [pl.BlockSpec(memory_space=pl.ANY)]
    chunk = kept((toks, 2 * HEAD_DIM), BF16)
    chunks = kept((2 * toks, 2 * HEAD_DIM), BF16)
    one = pl.BlockSpec(memory_space=pltpu.VMEM)
    o0, o1, o2, o3, own, dd, cumt, lead = pl.pallas_call(
        state_kernel,
        in_specs=smem(1) + vmem(7),
        out_specs=vmem(8),
        out_shape=[msg] * 4 + [chunk, kept((heads, toks), F32), kept((toks, heads), F32), kept((toks, heads), F32)],
        scratch_shapes=[pltpu.VMEM((NX, STATE + EXTRA, QUARTER), BF16)],
        compiler_params=params(12),
        cost_estimate=cost(30),
        name="chunk_states",
    )(*map(far, (rollout_lengths, mixer_input, input_map, step_raw, step_bias[None, :], decay_log[None, :],
                 key_heads, value_heads)))
    zs = [own, lax.ppermute(own, "ctx", z_shift(1))]
    came = [o0] + [lax.ppermute(o, "ctx", x_shift(k)) for k, o in ((1, o1), (2, o2), (3, o3))]

    y_local, token = pl.pallas_call(
        local_kernel,
        in_specs=smem(1) + vmem(6),
        out_specs=vmem(2),
        out_shape=[kept((toks, lanes), F32), kept((8, 128), F32)],
        compiler_params=params(12),
        cost_estimate=cost(25),
        name="within_chunk",
    )(rollout_lengths, near(mixer_input), near(input_map), near(output_map), *map(near, (dd, cumt)), skip_gain[None, :])

    sent = pl.pallas_call(
        relay_kernel, in_specs=vmem(1) + anywhere, out_specs=one, out_shape=chunk,
        compiler_params=params(4), cost_estimate=cost(5), name="relay",
    )(near(zs[1]), dd)
    for _ in range(3):
        sent = lax.ppermute(sent, "ctx", z_shift(1))
        zs.append(sent)
    soon = pl.pallas_call(
        join_kernel, in_specs=vmem(2), out_specs=one, out_shape=chunks,
        compiler_params=params(4), cost_estimate=cost(5), name="two_chunks",
    )(near(zs[1]), near(zs[2]))
    gs = [lax.ppermute(soon, "ctx", x_shift(k)) for k in (1, 2, 3)]
    prefix, total, pth = pl.pallas_call(
        row_kernel,
        in_specs=vmem(4) + [pl.BlockSpec(memory_space=pl.ANY)],
        out_specs=vmem(3),
        out_shape=[kept((NX, STATE, QUARTER), BF16), msg, kept((NX, 8, QUARTER), F32)],
        scratch_shapes=[pltpu.VMEM((NX, STATE + EXTRA, QUARTER), BF16)],
        compiler_params=params(8),
        cost_estimate=cost(10),
        name="row_scan",
    )(*map(near, came), token)

    once = lax.ppermute(total, "ctx", z_shift(1))
    pair = pl.pallas_call(
        pair_kernel,
        in_specs=vmem(2),
        out_specs=pl.BlockSpec(memory_space=pltpu.VMEM),
        out_shape=msg,
        compiler_params=params(4),
        cost_estimate=cost(5),
        name="two_rows",
    )(near(total), near(once))
    later = pl.pallas_call(
        edge_kernel, in_specs=vmem(3) + anywhere, out_specs=vmem(3), out_shape=[chunks] * 3,
        compiler_params=params(6), cost_estimate=cost(5), name="edge_chunks",
    )(near(own), near(zs[4]), near(zs[3]), pair)
    gs = gs + [lax.ppermute(a, "ctx", x_shift(k)) for k, a in zip((1, 2, 3), later)]

    twice = lax.ppermute(pair, "ctx", z_shift(1))
    before = lax.ppermute(twice, "ctx", z_shift(2))
    backs = pl.pallas_call(
        back_kernel,
        in_specs=vmem(4),
        out_specs=vmem(4),
        out_shape=[quarter] * 4,
        compiler_params=params(6),
        cost_estimate=cost(30),
        name="row_states",
    )(*map(near, (prefix, pth, twice, before)))
    incoming = [backs[0]] + [lax.ppermute(backs[k], "ctx", x_shift(k)) for k in (1, 2, 3)]

    q_heads = queries.shape[1] // HEAD_DIM
    acc, ml = pl.pallas_call(
        attend_first_kernel,
        in_specs=smem(1) + vmem(9) + anywhere,
        out_specs=vmem(2),
        out_shape=[kept((q_heads, toks, HEAD_DIM), F32)] * 2,
        scratch_shapes=attend_scratch(11, toks, q_heads),
        compiler_params=params(20),
        cost_estimate=cost(8),
        name="attend_first",
    )(rollout_lengths, queries, *map(near, (*zs, *gs[:3])), twice)
    attended = pl.pallas_call(
        attend_second_kernel,
        in_specs=smem(1) + vmem(6) + anywhere,
        out_specs=pl.BlockSpec(memory_space=pltpu.VMEM),
        out_shape=kept((q_heads, toks, HEAD_DIM), BF16),
        scratch_shapes=attend_scratch(6, toks, q_heads),
        compiler_params=params(14),
        cost_estimate=cost(5),
        name="attend_second",
    )(rollout_lengths, queries, *map(near, (*gs[3:], acc, ml)), twice)

    cols = out_weight.shape[1] // (2 * NY)
    send, keep = pl.pallas_call(
        project_kernel,
        in_specs=vmem(2) + anywhere,
        out_specs=vmem(2),
        out_shape=[kept((NY, toks, cols), BF16)] * 2,
        scratch_shapes=[pltpu.VMEM((toks, q_heads * HEAD_DIM), BF16), pltpu.VMEM((2, toks, cols), BF16)],
        compiler_params=params(8),
        cost_estimate=cost(3),
        name="project",
    )(near(attended), near(out_weight), pair)
    twin = lax.ppermute(send, "tp", TWIN)
    part = kept((toks, cols), BF16)
    mine, *summed = pl.pallas_call(
        add_kernel, in_specs=vmem(2), out_specs=vmem(NY), out_shape=[kept((toks, cols), F32)] + [part] * (NY - 1),
        compiler_params=params(6), cost_estimate=cost(0.5), name="two_cores",
    )(near(keep), near(twin))
    others = [lax.ppermute(a, "tp", y_shift(k)) for k, a in zip((1, 2, 3), summed)]
    block_out = pl.pallas_call(
        total_kernel, in_specs=vmem(NY), out_specs=one, out_shape=sds((toks, cols), BF16),
        compiler_params=params(6), cost_estimate=cost(0.5), name="four_rows",
    )(*map(near, (mine, *others)))

    mamba_out = pl.pallas_call(
        gate_kernel,
        in_specs=vmem(9),
        out_specs=pl.BlockSpec(memory_space=pltpu.VMEM),
        out_shape=sds((toks, lanes), BF16),
        scratch_shapes=[pltpu.VMEM((NX, STATE, QUARTER), BF16)],
        compiler_params=params(12),
        cost_estimate=cost(2.5),
        name="carry_gate_norm",
    )(*map(near, (y_local, output_map, lead, gate_input)), norm_gain[None, :], *map(near, incoming))
    return (mamba_out, block_out)


def solution(mesh):
    both = P("ctx", "tp")
    return jax.shard_map(
        body,
        mesh=mesh,
        in_specs=(both, both, both, both, P("tp", "ctx"), P("tp"), P("tp"), P("tp"), P("tp"),
                  both, both, both, P("tp", None), P()),
        out_specs=(both, both),
        check_vma=False,
    )
```

```python
import math

import jax
import jax.numpy as jnp
from jax import lax
from jax.experimental import pallas as pl
from jax.experimental.pallas import tpu as pltpu
from jax.sharding import PartitionSpec as P

HEAD_P = 64
STATE = 256
HEAD_DIM = 128
NZ = 8
NX = 4
NY = 4
LOG2E = math.log2(math.e)
EPS = 1e-05
BIG = -1e30
F32 = jnp.float32
BF16 = jnp.bfloat16
EXTRA = 16
QUARTER = 512


def iota(shape, dim):
    return lax.broadcasted_iota(jnp.int32, shape, dim)


def split3(a):
    hi = a.astype(BF16)
    rest = a - hi.astype(F32)
    mid = rest.astype(BF16)
    low = (rest - mid.astype(F32)).astype(BF16)
    return hi, mid, low


def spread(a, expand, terms=3):
    total = None
    for part in split3(a)[:terms]:
        one = jnp.dot(part, expand, preferred_element_type=F32)
        total = one if total is None else total + one
    return total


def expander(heads, lanes):
    return (iota((heads, lanes), 1) // HEAD_P == iota((heads, lanes), 0)).astype(F32).astype(BF16)


def place_of():
    ctx = lax.axis_index("ctx")
    return ctx // NX, lax.rem(ctx, NX)


def ends_of(lengths):
    e0 = lengths[0]
    e1 = e0 + lengths[1]
    e2 = e1 + lengths[2]
    return e0, e1, e2, e2 + lengths[3]


def rollout_at(pos, ends):
    count = jnp.zeros_like(pos)
    for e in ends:
        count = count + (pos >= e).astype(jnp.int32)
    return jnp.where(pos < 0, -1, count)


def pack_kernel(k_ref, v_ref, kv_ref):
    kv_ref[:, :HEAD_DIM] = k_ref[...]
    kv_ref[:, HEAD_DIM:] = v_ref[...]


def relay_kernel(a_ref, after, o_ref):
    o_ref[...] = a_ref[...]


def join_kernel(a_ref, b_ref, o_ref):
    rows = a_ref.shape[0]
    o_ref[:rows, :] = a_ref[...]
    o_ref[rows:, :] = b_ref[...]


def edge_kernel(own_ref, last_ref, b_ref, after, o1, o2, o3):
    xi = place_of()[1]
    rows = own_ref.shape[0]
    for k, out in ((1, o1), (2, o2), (3, o3)):
        out[rows:, :] = b_ref[...]

        @pl.when(xi + k < NX)
        def _():
            out[:rows, :] = own_ref[...]

        @pl.when(xi + k >= NX)
        def _():
            out[:rows, :] = last_ref[...]


def state_kernel(lengths, x_ref, b_ref, raw_ref, bias_ref, alog_ref, k_ref, v_ref,
                 o0, o1, o2, o3, kv_ref, d_ref, cumt_ref, lead_ref, scr):
    heads, toks = raw_ref.shape
    lanes = x_ref.shape[1]
    zi, xi = place_of()
    first = (zi * NX + xi) * toks
    ends = ends_of(lengths)
    kv_ref[:, :HEAD_DIM] = k_ref[...]
    kv_ref[:, HEAD_DIM:] = v_ref[...]
    width = jax.nn.softplus(raw_ref[...].T + bias_ref[...])
    rate2 = width * (-LOG2E * jnp.exp(alog_ref[...]))
    lower = (iota((toks, toks), 0) >= iota((toks, toks), 1)).astype(F32).astype(BF16)
    cumt = sum(jnp.dot(lower, part, preferred_element_type=F32) for part in split3(rate2))
    d_ref[...] = (cumt - jnp.log2(width)).T
    cumt_ref[...] = cumt
    before = rollout_at(first - 1, ends)
    last = rollout_at(first + (toks - 1), ends)
    roll = rollout_at(first + iota((toks, heads), 0), ends)
    lead_ref[...] = jnp.where(roll == before, jnp.exp2(cumt), 0.0)
    end = cumt[toks - 1:toks, :]
    tail = jnp.where(roll == last, jnp.exp2(end - cumt), 0.0) * width
    expand = expander(heads, lanes)
    xw = (spread(tail, expand, 2) * x_ref[...].astype(F32)).astype(BF16)
    state = lax.dot_general(b_ref[...], xw, (((0,), (0,)), ((), ())), preferred_element_type=F32)
    through = jnp.where(last == before, jnp.exp2(end), 0.0)
    th = [jnp.dot(part, expand, preferred_element_type=F32) for part in split3(through)]
    row = iota((EXTRA, lanes), 0)
    extra = jnp.where(row == 0, th[0], jnp.where(row == 1, th[1], jnp.where(row == 2, th[2], 0.0)))
    whole = jnp.concatenate([state, extra], axis=0).astype(BF16)
    for q in range(NX):
        scr[q] = whole[:, q * QUARTER:(q + 1) * QUARTER]
    for k, out in enumerate((o0, o1, o2, o3)):
        out[...] = scr[lax.rem(xi + k, NX)]


def with_decay(ref, state, decay):
    hi, mid, low = split3(decay)
    row = iota((EXTRA, QUARTER), 0)
    extra = jnp.where(row == 0, hi.astype(F32), jnp.where(row == 1, mid.astype(F32), jnp.where(row == 2, low.astype(F32), 0.0)))
    ref[:STATE, :] = state.astype(BF16)
    ref[STATE:, :] = extra.astype(BF16)


def decay_in(tail):
    tail = tail.astype(F32)
    return tail[0:1] + tail[1:2] + tail[2:3]


def row_kernel(a0, a1, a2, a3, after, p_ref, t_ref, pth_ref, scr):
    zi, xi = place_of()
    for k, a in enumerate((a0, a1, a2, a3)):
        scr[lax.rem(xi - k + NX, NX)] = a[...]
    total = jnp.zeros((STATE, QUARTER), F32)
    through = jnp.ones((1, QUARTER), F32)
    for j in range(NX):
        p_ref[j] = total.astype(BF16)
        pth_ref[j] = jnp.broadcast_to(through, (8, QUARTER))
        one = decay_in(scr[j, STATE:STATE + EXTRA, :])
        total = one * total + scr[j, :STATE, :].astype(F32)
        through = through * one
    with_decay(t_ref, total, jnp.where(zi > 0, through, 0.0))


def pair_kernel(t_ref, came_ref, o_ref):
    through = decay_in(t_ref[STATE:, :])
    total = t_ref[:STATE, :].astype(F32) + through * came_ref[:STATE, :].astype(F32)
    with_decay(o_ref, total, through * decay_in(came_ref[STATE:, :]))


def back_kernel(p_ref, pth_ref, near_ref, far_ref, o0, o1, o2, o3):
    zi, xi = place_of()
    came = near_ref[:STATE, :].astype(F32) + decay_in(near_ref[STATE:, :]) * far_ref[:STATE, :].astype(F32)
    came = jnp.where(zi > 0, came, 0.0)
    for k, out in enumerate((o0, o1, o2, o3)):
        j = lax.rem(xi + k, NX)
        out[...] = (p_ref[j].astype(F32) + pth_ref[j][0:1] * came).astype(BF16)


def local_kernel(lengths, x_ref, b_ref, c_ref, d_ref, cumt_ref, skip_ref, y_ref, token_ref):
    token_ref[...] = jnp.zeros_like(token_ref)
    toks, lanes = x_ref.shape
    heads = d_ref.shape[0]
    half = toks // 2
    zi, xi = place_of()
    first = (zi * NX + xi) * toks
    ends = ends_of(lengths)
    roll_t = rollout_at(first + iota((toks, toks), 0), ends)
    roll_s = rollout_at(first + iota((toks, toks), 1), ends)
    seen = (roll_t == roll_s) & (iota((toks, toks), 0) >= iota((toks, toks), 1))
    inner = lax.dot_general(c_ref[...], b_ref[...], (((1,), (1,)), ((), ())), preferred_element_type=F32)
    inner = jnp.where(seen, inner, 0.0)
    left = iota((half, 128), 1) < HEAD_P
    skip = spread(skip_ref[...], expander(heads, lanes))
    d_all = d_ref[...]
    cumt = cumt_ref[...]
    for pair in range(heads // 2):
        cols = slice(pair * 128, (pair + 1) * 128)
        x_pair = x_ref[:, cols]
        for rows, width in ((slice(0, half), half), (slice(half, toks), toks)):
            res = []
            for h in (2 * pair, 2 * pair + 1):
                diff = cumt[rows, h:h + 1] - d_all[h:h + 1, :width]
                mix = (jnp.exp2(jnp.minimum(diff, 64.0)) * inner[rows, :width]).astype(BF16)
                res.append(jnp.dot(mix, x_pair[:width], preferred_element_type=F32))
            y_ref[rows, cols] = jnp.where(left, res[0], res[1]) + skip[:, cols] * x_pair[rows].astype(F32)


def gate_kernel(y_ref, c_ref, lead_ref, gate_ref, gain_ref, i0, i1, i2, i3, out_ref, scr):
    toks, lanes = y_ref.shape
    heads = lead_ref.shape[1]
    xi = place_of()[1]
    for k, a in enumerate((i0, i1, i2, i3)):
        scr[lax.rem(xi - k + NX, NX)] = a[...]
    expand = expander(heads, lanes)
    square = jnp.zeros((toks, 1), F32)
    held = []
    for q in range(NX):
        cols = slice(q * QUARTER, (q + 1) * QUARTER)
        carried = jnp.dot(c_ref[...], scr[q], preferred_element_type=F32)
        lead = spread(lead_ref[...], expand[:, cols], 2)
        v = gate_ref[:, cols].astype(F32)
        gated = (y_ref[:, cols] + lead * carried) * (v / (1.0 + jnp.exp(-v)))
        square = square + jnp.sum(gated * gated, axis=1, keepdims=True)
        held.append(gated)
    factor = lax.rsqrt(square * (1.0 / lanes) + EPS)
    for q in range(NX):
        cols = slice(q * QUARTER, (q + 1) * QUARTER)
        out_ref[:, cols] = (held[q] * factor * gain_ref[:, cols]).astype(BF16)


def fill(lengths, first, slots, k_buf, v_buf):
    toks = k_buf.shape[1]
    lane = iota((toks, HEAD_DIM), 1)
    row = iota((toks, HEAD_DIM), 0)
    ones = (lane == 0).astype(F32).astype(BF16)
    ends = ends_of(lengths)
    begins = (0,) + ends[:3]
    lane_row = iota((1, HEAD_DIM), 1)
    low = jnp.zeros((1, HEAD_DIM), jnp.int32)
    high = low
    for r in range(4):
        low = jnp.where(lane_row == r, begins[r], low)
        high = jnp.where(lane_row == r, ends[r], high)
    for i, (slot, kv) in enumerate(slots):
        start = first + (slot - 16) * toks
        k_buf[i, :, :HEAD_DIM] = kv[:, :HEAD_DIM]
        v_buf[i, :, :HEAD_DIM] = kv[:, HEAD_DIM:]
        k_buf[i, :, HEAD_DIM:] = jnp.where((row >= low - start) & (row < high - start), 0.0, BIG).astype(BF16)
        v_buf[i, :, HEAD_DIM:] = ones


def fill_queries(ends, first, q_ref, q_buf):
    toks = q_ref.shape[0]
    lane = iota((toks, HEAD_DIM), 1)
    mine = (rollout_at(first + iota((toks, 1), 0), ends) == lane).astype(F32).astype(BF16)
    for h in range(q_ref.shape[1] // HEAD_DIM):
        rows = slice(h % 2 * toks, (h % 2 + 1) * toks)
        q_buf[h // 2, rows, :HEAD_DIM] = q_ref[:, h * HEAD_DIM:(h + 1) * HEAD_DIM]
        q_buf[h // 2, rows, HEAD_DIM:] = mine


def over_heads(heads, chunks, q_buf, k_buf, v_buf, s_a, s_b, causal_at, start, finish):
    rows, toks = q_buf.shape[1], k_buf.shape[1]
    scale = LOG2E / math.sqrt(HEAD_DIM)
    causal = iota((rows, toks), 0) % toks >= iota((rows, toks), 1)

    def scores(h, buf, j, peak):
        s = lax.dot_general(q_buf[h], k_buf[j], (((1,), (1,)), ((), ())), preferred_element_type=F32)
        if j == causal_at:
            s = jnp.where(causal, s, BIG)
        buf[j] = s
        return jnp.maximum(peak, jnp.maximum(s[:, :128], s[:, 128:]))

    def both(h, buf_now, buf_next, peak):
        top = jnp.max(peak, axis=1, keepdims=True)
        acc = start[1](h, top, scale)
        nxt = jnp.minimum(h + 1, heads - 1)
        peak = start[0](nxt)
        for j in range(chunks):
            peak = scores(nxt, buf_next, j, peak)
            p = jnp.exp2((buf_now[j] - top) * scale).astype(BF16)
            acc = acc + jnp.dot(p, v_buf[j], preferred_element_type=F32)
        finish(h, top, acc)
        return peak

    def two(i, peak):
        peak = both(2 * i, s_a, s_b, peak)
        return both(2 * i + 1, s_b, s_a, peak)

    peak = start[0](0)
    for j in range(chunks):
        peak = scores(0, s_a, j, peak)
    lax.fori_loop(0, heads // 2, two, peak)


def two_of(ref, h):
    return jnp.concatenate([ref[2 * h], ref[2 * h + 1]], axis=0)


def attend_scratch(chunks, toks, heads):
    wide = pltpu.VMEM((chunks, toks, 2 * HEAD_DIM), BF16)
    logits = pltpu.VMEM((chunks, 2 * toks, toks), F32)
    return [wide, wide, pltpu.VMEM((heads // 2, 2 * toks, 2 * HEAD_DIM), BF16), logits, logits]


def attend_first_kernel(lengths, q_ref, own, z1, z2, z3, z4, g1, g2, g3, after, acc_ref, ml_ref,
                        k_buf, v_buf, q_buf, s_a, s_b):
    pairs, rows = q_buf.shape[:2]
    toks = q_ref.shape[0]
    zi, xi = place_of()
    first = (zi * NX + xi) * toks
    ends = ends_of(lengths)
    slots = [(16, own), (12, z1), (8, z2), (4, z3), (0, z4)]
    for k, g in ((1, g1), (2, g2), (3, g3)):
        ahead = xi >= k
        slots.append((jnp.where(ahead, 12 - k, 16 - k), g[0:toks, :]))
        slots.append((jnp.where(ahead, 8 - k, 12 - k), g[toks:2 * toks, :]))
    fill(lengths, first, slots, k_buf, v_buf)
    fill_queries(ends, first, q_ref, q_buf)
    lane = iota((rows, HEAD_DIM), 1)

    def finish(h, top, acc):
        ml = jnp.where(lane == 0, acc[:, HEAD_DIM:], top)
        for i in range(2):
            acc_ref[2 * h + i] = acc[i * toks:(i + 1) * toks, :HEAD_DIM]
            ml_ref[2 * h + i] = ml[i * toks:(i + 1) * toks]

    start = (lambda h: jnp.full((rows, HEAD_DIM), BIG, F32),
             lambda h, top, scale: jnp.zeros((rows, 2 * HEAD_DIM), F32))
    over_heads(pairs, len(slots), q_buf, k_buf, v_buf, s_a, s_b, 0, start, finish)


def attend_second_kernel(lengths, q_ref, g1, g2, g3, acc_ref, ml_ref, after, out_ref,
                         k_buf, v_buf, q_buf, s_a, s_b):
    pairs, rows = q_buf.shape[:2]
    toks = q_ref.shape[0]
    zi, xi = place_of()
    first = (zi * NX + xi) * toks
    ends = ends_of(lengths)
    slots = []
    for k, g in ((1, g1), (2, g2), (3, g3)):
        ahead = xi >= k
        slots.append((jnp.where(ahead, 16 - k, 4 - k), g[0:toks, :]))
        slots.append((jnp.where(ahead, 4 - k, 8 - k), g[toks:2 * toks, :]))
    fill(lengths, first, slots, k_buf, v_buf)
    fill_queries(ends, first, q_ref, q_buf)
    lane = iota((rows, HEAD_DIM), 1)

    def begin(h, top, scale):
        ml = two_of(ml_ref, h)
        old = jnp.exp2((ml[:, 1:2] - top) * scale)
        total = jnp.where(lane == 0, ml, 0.0)
        return jnp.concatenate([two_of(acc_ref, h), total], axis=1) * old

    def finish(h, top, acc):
        res = acc[:, :HEAD_DIM] / acc[:, HEAD_DIM:HEAD_DIM + 1]
        for i in range(2):
            out_ref[2 * h + i] = res[i * toks:(i + 1) * toks].astype(BF16)

    start = (lambda h: jnp.where(lane == 0, BIG, two_of(ml_ref, h)), begin)
    over_heads(pairs, len(slots), q_buf, k_buf, v_buf, s_a, s_b, None, start, finish)


def project_kernel(a_ref, w_ref, after, send_ref, keep_ref, wide, both):
    h = a_ref.shape[0]
    cols = both.shape[2]
    tp = lax.axis_index("tp")
    y, core = tp // 2, lax.rem(tp, 2)
    for i in range(h):
        wide[:, i * HEAD_DIM:(i + 1) * HEAD_DIM] = a_ref[i]
    for k in range(NY):
        at = pl.multiple_of(lax.rem(y + k, NY) * (2 * cols), 2 * cols)
        for c in range(2):
            both[c] = jnp.dot(wide[...], w_ref[:, pl.ds(at + c * cols, cols)], preferred_element_type=F32).astype(BF16)
        send_ref[k] = both[1 - core]
        keep_ref[k] = both[core]


def add_kernel(keep_ref, twin_ref, first_ref, *out_refs):
    first_ref[...] = keep_ref[0].astype(F32) + twin_ref[0].astype(F32)
    for k, out in enumerate(out_refs):
        out[...] = (keep_ref[k + 1].astype(F32) + twin_ref[k + 1].astype(F32)).astype(BF16)


def total_kernel(first_ref, a_ref, b_ref, c_ref, out_ref):
    total = first_ref[...] + a_ref[...].astype(F32)
    out_ref[...] = (total + b_ref[...].astype(F32) + c_ref[...].astype(F32)).astype(BF16)


def vmem(n):
    return [pl.BlockSpec(memory_space=pltpu.VMEM)] * n


def smem(n):
    return [pl.BlockSpec(memory_space=pltpu.SMEM)] * n


def cost(us):
    return pl.CostEstimate(flops=int(us * 1.1e9), transcendentals=0, bytes_accessed=int(us * 3.2e6))


def kept(shape, dtype):
    return pltpu.VMEM(shape, dtype)


def sds(shape, dtype):
    return jax.ShapeDtypeStruct(shape, dtype)


def far(a):
    return pltpu.with_memory_space_constraint(a, pltpu.HBM)


def params(mib):
    return pltpu.CompilerParams(vmem_limit_bytes=mib * 1024 * 1024)


def near(a):
    return pltpu.with_memory_space_constraint(a, pltpu.VMEM)


def x_shift(k):
    return [(NX * z + x, NX * z + (x + k) % NX) for z in range(NZ) for x in range(NX)]


def y_shift(k):
    return [(2 * y + c, 2 * ((y + k) % NY) + c) for y in range(NY) for c in range(2)]


def z_shift(k):
    return [(NX * z + x, NX * ((z + k) % NZ) + x) for z in range(NZ) for x in range(NX)]


TWIN = [(i, i ^ 1) for i in range(2 * NY)]


def body(mixer_input, gate_input, input_map, output_map, step_raw, step_bias, decay_log, skip_gain,
         norm_gain, queries, key_heads, value_heads, out_weight, rollout_lengths):
    toks, lanes = mixer_input.shape
    heads = step_raw.shape[0]
    msg = kept((STATE + EXTRA, QUARTER), BF16)
    quarter = kept((STATE, QUARTER), BF16)

    anywhere = [pl.BlockSpec(memory_space=pl.ANY)]
    chunk = kept((toks, 2 * HEAD_DIM), BF16)
    chunks = kept((2 * toks, 2 * HEAD_DIM), BF16)
    one = pl.BlockSpec(memory_space=pltpu.VMEM)
    o0, o1, o2, o3, own, dd, cumt, lead = pl.pallas_call(
        state_kernel,
        in_specs=smem(1) + vmem(7),
        out_specs=vmem(8),
        out_shape=[msg] * 4 + [chunk, kept((heads, toks), F32), kept((toks, heads), F32), kept((toks, heads), F32)],
        scratch_shapes=[pltpu.VMEM((NX, STATE + EXTRA, QUARTER), BF16)],
        compiler_params=params(12),
        cost_estimate=cost(30),
        name="chunk_states",
    )(*map(far, (rollout_lengths, mixer_input, input_map, step_raw, step_bias[None, :], decay_log[None, :],
                 key_heads, value_heads)))
    zs = [own, lax.ppermute(own, "ctx", z_shift(1))]
    came = [o0] + [lax.ppermute(o, "ctx", x_shift(k)) for k, o in ((1, o1), (2, o2), (3, o3))]

    y_local, token = pl.pallas_call(
        local_kernel,
        in_specs=smem(1) + vmem(6),
        out_specs=vmem(2),
        out_shape=[kept((toks, lanes), F32), kept((8, 128), F32)],
        compiler_params=params(12),
        cost_estimate=cost(25),
        name="within_chunk",
    )(rollout_lengths, near(mixer_input), near(input_map), near(output_map), *map(near, (dd, cumt)), skip_gain[None, :])

    sent = pl.pallas_call(
        relay_kernel, in_specs=vmem(1) + anywhere, out_specs=one, out_shape=chunk,
        compiler_params=params(4), cost_estimate=cost(5), name="relay",
    )(near(zs[1]), dd)
    for _ in range(3):
        sent = lax.ppermute(sent, "ctx", z_shift(1))
        zs.append(sent)
    soon = pl.pallas_call(
        join_kernel, in_specs=vmem(2), out_specs=one, out_shape=chunks,
        compiler_params=params(4), cost_estimate=cost(5), name="two_chunks",
    )(near(zs[1]), near(zs[2]))
    gs = [lax.ppermute(soon, "ctx", x_shift(k)) for k in (1, 2, 3)]
    prefix, total, pth = pl.pallas_call(
        row_kernel,
        in_specs=vmem(4) + [pl.BlockSpec(memory_space=pl.ANY)],
        out_specs=vmem(3),
        out_shape=[kept((NX, STATE, QUARTER), BF16), msg, kept((NX, 8, QUARTER), F32)],
        scratch_shapes=[pltpu.VMEM((NX, STATE + EXTRA, QUARTER), BF16)],
        compiler_params=params(8),
        cost_estimate=cost(10),
        name="row_scan",
    )(*map(near, came), token)

    once = lax.ppermute(total, "ctx", z_shift(1))
    pair = pl.pallas_call(
        pair_kernel,
        in_specs=vmem(2),
        out_specs=pl.BlockSpec(memory_space=pltpu.VMEM),
        out_shape=msg,
        compiler_params=params(4),
        cost_estimate=cost(5),
        name="two_rows",
    )(near(total), near(once))
    later = pl.pallas_call(
        edge_kernel, in_specs=vmem(3) + anywhere, out_specs=vmem(3), out_shape=[chunks] * 3,
        compiler_params=params(6), cost_estimate=cost(5), name="edge_chunks",
    )(near(own), near(zs[4]), near(zs[3]), pair)
    gs = gs + [lax.ppermute(a, "ctx", x_shift(k)) for k, a in zip((1, 2, 3), later)]

    twice = lax.ppermute(pair, "ctx", z_shift(1))
    before = lax.ppermute(twice, "ctx", z_shift(2))
    backs = pl.pallas_call(
        back_kernel,
        in_specs=vmem(4),
        out_specs=vmem(4),
        out_shape=[quarter] * 4,
        compiler_params=params(6),
        cost_estimate=cost(30),
        name="row_states",
    )(*map(near, (prefix, pth, twice, before)))
    incoming = [backs[0]] + [lax.ppermute(backs[k], "ctx", x_shift(k)) for k in (1, 2, 3)]

    q_heads = queries.shape[1] // HEAD_DIM
    acc, ml = pl.pallas_call(
        attend_first_kernel,
        in_specs=smem(1) + vmem(9) + anywhere,
        out_specs=vmem(2),
        out_shape=[kept((q_heads, toks, HEAD_DIM), F32)] * 2,
        scratch_shapes=attend_scratch(11, toks, q_heads),
        compiler_params=params(20),
        cost_estimate=cost(8),
        name="attend_first",
    )(rollout_lengths, queries, *map(near, (*zs, *gs[:3])), twice)
    attended = pl.pallas_call(
        attend_second_kernel,
        in_specs=smem(1) + vmem(6) + anywhere,
        out_specs=pl.BlockSpec(memory_space=pltpu.VMEM),
        out_shape=kept((q_heads, toks, HEAD_DIM), BF16),
        scratch_shapes=attend_scratch(6, toks, q_heads),
        compiler_params=params(14),
        cost_estimate=cost(5),
        name="attend_second",
    )(rollout_lengths, queries, *map(near, (*gs[3:], acc, ml)), twice)

    cols = out_weight.shape[1] // (2 * NY)
    send, keep = pl.pallas_call(
        project_kernel,
        in_specs=vmem(2) + anywhere,
        out_specs=vmem(2),
        out_shape=[kept((NY, toks, cols), BF16)] * 2,
        scratch_shapes=[pltpu.VMEM((toks, q_heads * HEAD_DIM), BF16), pltpu.VMEM((2, toks, cols), BF16)],
        compiler_params=params(8),
        cost_estimate=cost(3),
        name="project",
    )(near(attended), near(out_weight), pair)
    twin = lax.ppermute(send, "tp", TWIN)
    part = kept((toks, cols), BF16)
    mine, *summed = pl.pallas_call(
        add_kernel, in_specs=vmem(2), out_specs=vmem(NY), out_shape=[kept((toks, cols), F32)] + [part] * (NY - 1),
        compiler_params=params(6), cost_estimate=cost(0.5), name="two_cores",
    )(near(keep), near(twin))
    others = [lax.ppermute(a, "tp", y_shift(k)) for k, a in zip((1, 2, 3), summed)]
    block_out = pl.pallas_call(
        total_kernel, in_specs=vmem(NY), out_specs=one, out_shape=sds((toks, cols), BF16),
        compiler_params=params(6), cost_estimate=cost(0.5), name="four_rows",
    )(*map(near, (mine, *others)))

    mamba_out = pl.pallas_call(
        gate_kernel,
        in_specs=vmem(9),
        out_specs=pl.BlockSpec(memory_space=pltpu.VMEM),
        out_shape=sds((toks, lanes), BF16),
        scratch_shapes=[pltpu.VMEM((NX, STATE, QUARTER), BF16)],
        compiler_params=params(12),
        cost_estimate=cost(2.5),
        name="carry_gate_norm",
    )(*map(near, (y_local, output_map, lead, gate_input)), norm_gain[None, :], *map(near, incoming))
    return (mamba_out, block_out)


def solution(mesh):
    both = P("ctx", "tp")
    return jax.shard_map(
        body,
        mesh=mesh,
        in_specs=(both, both, both, both, P("tp", "ctx"), P("tp"), P("tp"), P("tp"), P("tp"),
                  both, both, both, P("tp", None), P()),
        out_specs=(both, both),
        check_vma=False,
    )
```

```python
import math

import jax
import jax.numpy as jnp
from jax import lax
from jax.experimental import pallas as pl
from jax.experimental.pallas import tpu as pltpu
from jax.sharding import PartitionSpec as P

HEAD_P = 64
STATE = 256
HEAD_DIM = 128
NZ = 8
NX = 4
NY = 4
LOG2E = math.log2(math.e)
EPS = 1e-05
BIG = -1e30
F32 = jnp.float32
BF16 = jnp.bfloat16
EXTRA = 16
QUARTER = 512


def iota(shape, dim):
    return lax.broadcasted_iota(jnp.int32, shape, dim)


def split3(a):
    hi = a.astype(BF16)
    rest = a - hi.astype(F32)
    mid = rest.astype(BF16)
    low = (rest - mid.astype(F32)).astype(BF16)
    return hi, mid, low


def spread(a, expand, terms=3):
    total = None
    for part in split3(a)[:terms]:
        one = jnp.dot(part, expand, preferred_element_type=F32)
        total = one if total is None else total + one
    return total


def expander(heads, lanes):
    return (iota((heads, lanes), 1) // HEAD_P == iota((heads, lanes), 0)).astype(F32).astype(BF16)


def place_of():
    ctx = lax.axis_index("ctx")
    return ctx // NX, lax.rem(ctx, NX)


def ends_of(lengths):
    e0 = lengths[0]
    e1 = e0 + lengths[1]
    e2 = e1 + lengths[2]
    return e0, e1, e2, e2 + lengths[3]


def rollout_at(pos, ends):
    count = jnp.zeros_like(pos)
    for e in ends:
        count = count + (pos >= e).astype(jnp.int32)
    return jnp.where(pos < 0, -1, count)


def pack_kernel(k_ref, v_ref, kv_ref):
    kv_ref[:, :HEAD_DIM] = k_ref[...]
    kv_ref[:, HEAD_DIM:] = v_ref[...]


def relay_kernel(a_ref, after, o_ref):
    o_ref[...] = a_ref[...]


def join_kernel(a_ref, b_ref, o_ref):
    rows = a_ref.shape[0]
    o_ref[:rows, :] = a_ref[...]
    o_ref[rows:, :] = b_ref[...]


def edge_kernel(own_ref, last_ref, b_ref, after, o1, o2, o3):
    xi = place_of()[1]
    rows = own_ref.shape[0]
    for k, out in ((1, o1), (2, o2), (3, o3)):
        out[rows:, :] = b_ref[...]

        @pl.when(xi + k < NX)
        def _():
            out[:rows, :] = own_ref[...]

        @pl.when(xi + k >= NX)
        def _():
            out[:rows, :] = last_ref[...]


def state_kernel(lengths, x_ref, b_ref, raw_ref, bias_ref, alog_ref, k_ref, v_ref,
                 o0, o1, o2, o3, kv_ref, d_ref, cumt_ref, lead_ref, scr):
    heads, toks = raw_ref.shape
    lanes = x_ref.shape[1]
    zi, xi = place_of()
    first = (zi * NX + xi) * toks
    ends = ends_of(lengths)
    kv_ref[:, :HEAD_DIM] = k_ref[...]
    kv_ref[:, HEAD_DIM:] = v_ref[...]
    width = jax.nn.softplus(raw_ref[...].T + bias_ref[...])
    rate2 = width * (-LOG2E * jnp.exp(alog_ref[...]))
    lower = (iota((toks, toks), 0) >= iota((toks, toks), 1)).astype(F32).astype(BF16)
    cumt = sum(jnp.dot(lower, part, preferred_element_type=F32) for part in split3(rate2))
    d_ref[...] = (cumt - jnp.log2(width)).T
    cumt_ref[...] = cumt
    before = rollout_at(first - 1, ends)
    last = rollout_at(first + (toks - 1), ends)
    roll = rollout_at(first + iota((toks, heads), 0), ends)
    lead_ref[...] = jnp.where(roll == before, jnp.exp2(cumt), 0.0)
    end = cumt[toks - 1:toks, :]
    tail = jnp.where(roll == last, jnp.exp2(end - cumt), 0.0) * width
    expand = expander(heads, lanes)
    xw = (spread(tail, expand, 2) * x_ref[...].astype(F32)).astype(BF16)
    state = lax.dot_general(b_ref[...], xw, (((0,), (0,)), ((), ())), preferred_element_type=F32)
    through = jnp.where(last == before, jnp.exp2(end), 0.0)
    th = [jnp.dot(part, expand, preferred_element_type=F32) for part in split3(through)]
    row = iota((EXTRA, lanes), 0)
    extra = jnp.where(row == 0, th[0], jnp.where(row == 1, th[1], jnp.where(row == 2, th[2], 0.0)))
    whole = jnp.concatenate([state, extra], axis=0).astype(BF16)
    for q in range(NX):
        scr[q] = whole[:, q * QUARTER:(q + 1) * QUARTER]
    for k, out in enumerate((o0, o1, o2, o3)):
        out[...] = scr[lax.rem(xi + k, NX)]


def with_decay(ref, state, decay):
    hi, mid, low = split3(decay)
    row = iota((EXTRA, QUARTER), 0)
    extra = jnp.where(row == 0, hi.astype(F32), jnp.where(row == 1, mid.astype(F32), jnp.where(row == 2, low.astype(F32), 0.0)))
    ref[:STATE, :] = state.astype(BF16)
    ref[STATE:, :] = extra.astype(BF16)


def decay_in(tail):
    tail = tail.astype(F32)
    return tail[0:1] + tail[1:2] + tail[2:3]


def row_kernel(a0, a1, a2, a3, after, p_ref, t_ref, pth_ref, scr):
    zi, xi = place_of()
    for k, a in enumerate((a0, a1, a2, a3)):
        scr[lax.rem(xi - k + NX, NX)] = a[...]
    total = jnp.zeros((STATE, QUARTER), F32)
    through = jnp.ones((1, QUARTER), F32)
    for j in range(NX):
        p_ref[j] = total.astype(BF16)
        pth_ref[j] = jnp.broadcast_to(through, (8, QUARTER))
        one = decay_in(scr[j, STATE:STATE + EXTRA, :])
        total = one * total + scr[j, :STATE, :].astype(F32)
        through = through * one
    with_decay(t_ref, total, jnp.where(zi > 0, through, 0.0))


def pair_kernel(t_ref, came_ref, o_ref):
    through = decay_in(t_ref[STATE:, :])
    total = t_ref[:STATE, :].astype(F32) + through * came_ref[:STATE, :].astype(F32)
    with_decay(o_ref, total, through * decay_in(came_ref[STATE:, :]))


def back_kernel(p_ref, pth_ref, near_ref, far_ref, o0, o1, o2, o3):
    zi, xi = place_of()
    came = near_ref[:STATE, :].astype(F32) + decay_in(near_ref[STATE:, :]) * far_ref[:STATE, :].astype(F32)
    came = jnp.where(zi > 0, came, 0.0)
    for k, out in enumerate((o0, o1, o2, o3)):
        j = lax.rem(xi + k, NX)
        out[...] = (p_ref[j].astype(F32) + pth_ref[j][0:1] * came).astype(BF16)


def local_kernel(lengths, x_ref, b_ref, c_ref, d_ref, cumt_ref, skip_ref, y_ref, token_ref, cum_scr, skip_scr):
    token_ref[...] = jnp.zeros_like(token_ref)
    toks, lanes = x_ref.shape
    heads = d_ref.shape[0]
    half = toks // 2
    zi, xi = place_of()
    first = (zi * NX + xi) * toks
    ends = ends_of(lengths)
    roll_t = rollout_at(first + iota((toks, toks), 0), ends)
    roll_s = rollout_at(first + iota((toks, toks), 1), ends)
    seen = (roll_t == roll_s) & (iota((toks, toks), 0) >= iota((toks, toks), 1))
    inner = lax.dot_general(c_ref[...], b_ref[...], (((1,), (1,)), ((), ())), preferred_element_type=F32)
    inner = jnp.where(seen, inner, 0.0)
    left = iota((half, 128), 1) < HEAD_P
    skip = spread(skip_ref[...], expander(heads, lanes))
    group = 8
    wide = group * HEAD_P
    for g in range(heads // group):
        cum_scr[g] = cumt_ref[:, g * group:(g + 1) * group]
        skip_scr[g] = skip[:, g * wide:(g + 1) * wide]

    def some(g, carry):
        cumt, d_all, gain = cum_scr[g], d_ref[pl.ds(pl.multiple_of(g * group, group), group), :], skip_scr[g]
        base = pl.multiple_of(g * wide, wide)
        for pair in range(group // 2):
            cols = pl.ds(base + pair * 128, 128)
            x_pair = x_ref[:, cols]
            gains = gain[:, pair * 128:(pair + 1) * 128]
            for rows, width in ((slice(0, half), half), (slice(half, toks), toks)):
                res = []
                for h in (2 * pair, 2 * pair + 1):
                    diff = cumt[rows, h:h + 1] - d_all[h:h + 1, :width]
                    mix = (jnp.exp2(jnp.minimum(diff, 64.0)) * inner[rows, :width]).astype(BF16)
                    res.append(jnp.dot(mix, x_pair[:width], preferred_element_type=F32))
                y_ref[rows, cols] = jnp.where(left, res[0], res[1]) + gains * x_pair[rows].astype(F32)
        return carry

    lax.fori_loop(0, heads // group, some, 0)


def gate_kernel(y_ref, c_ref, lead_ref, gate_ref, gain_ref, i0, i1, i2, i3, out_ref, scr):
    toks, lanes = y_ref.shape
    heads = lead_ref.shape[1]
    xi = place_of()[1]
    for k, a in enumerate((i0, i1, i2, i3)):
        scr[lax.rem(xi - k + NX, NX)] = a[...]
    expand = expander(heads, lanes)
    square = jnp.zeros((toks, 1), F32)
    held = []
    for q in range(NX):
        cols = slice(q * QUARTER, (q + 1) * QUARTER)
        carried = jnp.dot(c_ref[...], scr[q], preferred_element_type=F32)
        lead = spread(lead_ref[...], expand[:, cols], 2)
        v = gate_ref[:, cols].astype(F32)
        gated = (y_ref[:, cols] + lead * carried) * (v / (1.0 + jnp.exp(-v)))
        square = square + jnp.sum(gated * gated, axis=1, keepdims=True)
        held.append(gated)
    factor = lax.rsqrt(square * (1.0 / lanes) + EPS)
    for q in range(NX):
        cols = slice(q * QUARTER, (q + 1) * QUARTER)
        out_ref[:, cols] = (held[q] * factor * gain_ref[:, cols]).astype(BF16)


def fill(lengths, first, slots, k_buf, v_buf):
    toks = k_buf.shape[1]
    lane = iota((toks, HEAD_DIM), 1)
    row = iota((toks, HEAD_DIM), 0)
    ones = (lane == 0).astype(F32).astype(BF16)
    ends = ends_of(lengths)
    begins = (0,) + ends[:3]
    lane_row = iota((1, HEAD_DIM), 1)
    low = jnp.zeros((1, HEAD_DIM), jnp.int32)
    high = low
    for r in range(4):
        low = jnp.where(lane_row == r, begins[r], low)
        high = jnp.where(lane_row == r, ends[r], high)
    for i, (slot, kv) in enumerate(slots):
        start = first + (slot - 16) * toks
        k_buf[i, :, :HEAD_DIM] = kv[:, :HEAD_DIM]
        v_buf[i, :, :HEAD_DIM] = kv[:, HEAD_DIM:]
        k_buf[i, :, HEAD_DIM:] = jnp.where((row >= low - start) & (row < high - start), 0.0, BIG).astype(BF16)
        v_buf[i, :, HEAD_DIM:] = ones


def fill_queries(ends, first, q_ref, q_buf):
    toks = q_ref.shape[0]
    lane = iota((toks, HEAD_DIM), 1)
    mine = (rollout_at(first + iota((toks, 1), 0), ends) == lane).astype(F32).astype(BF16)
    for h in range(q_ref.shape[1] // HEAD_DIM):
        rows = slice(h % 2 * toks, (h % 2 + 1) * toks)
        q_buf[h // 2, rows, :HEAD_DIM] = q_ref[:, h * HEAD_DIM:(h + 1) * HEAD_DIM]
        q_buf[h // 2, rows, HEAD_DIM:] = mine


def over_heads(heads, chunks, q_buf, k_buf, v_buf, s_a, s_b, causal_at, start, finish, peel):
    rows, toks = q_buf.shape[1], k_buf.shape[1]
    scale = LOG2E / math.sqrt(HEAD_DIM)
    causal = iota((rows, toks), 0) % toks >= iota((rows, toks), 1)

    def scores(h, buf, j, peak):
        s = lax.dot_general(q_buf[h], k_buf[j], (((1,), (1,)), ((), ())), preferred_element_type=F32)
        if j == causal_at:
            s = jnp.where(causal, s, BIG)
        buf[j] = s
        return jnp.maximum(peak, jnp.maximum(s[:, :128], s[:, 128:]))

    def both(h, buf_now, buf_next, peak, more=True):
        nxt = h + 1 if peel else jnp.minimum(h + 1, heads - 1)
        top = jnp.max(peak, axis=1, keepdims=True)
        acc = start[1](h, top, scale)
        if more:
            peak = start[0](nxt)
        for j in range(chunks):
            if more:
                peak = scores(nxt, buf_next, j, peak)
            p = jnp.exp2((buf_now[j] - top) * scale).astype(BF16)
            acc = acc + jnp.dot(p, v_buf[j], preferred_element_type=F32)
        finish(h, top, acc)
        return peak

    def two(i, peak):
        peak = both(2 * i, s_a, s_b, peak)
        return both(2 * i + 1, s_b, s_a, peak)

    peak = start[0](0)
    for j in range(chunks):
        peak = scores(0, s_a, j, peak)
    peak = lax.fori_loop(0, heads // 2 - (1 if peel else 0), two, peak)
    if peel:
        peak = both(heads - 2, s_a, s_b, peak)
        both(heads - 1, s_b, s_a, peak, False)


def two_of(ref, h):
    return jnp.concatenate([ref[2 * h], ref[2 * h + 1]], axis=0)


def attend_scratch(chunks, toks, heads):
    wide = pltpu.VMEM((chunks, toks, 2 * HEAD_DIM), BF16)
    logits = pltpu.VMEM((chunks, 2 * toks, toks), F32)
    return [wide, wide, pltpu.VMEM((heads // 2, 2 * toks, 2 * HEAD_DIM), BF16), logits, logits]


def attend_first_kernel(lengths, q_ref, own, z1, z2, z3, z4, g1, g2, g3, after, acc_ref, ml_ref,
                        k_buf, v_buf, q_buf, s_a, s_b):
    pairs, rows = q_buf.shape[:2]
    toks = q_ref.shape[0]
    zi, xi = place_of()
    first = (zi * NX + xi) * toks
    ends = ends_of(lengths)
    slots = [(16, own), (12, z1), (8, z2), (4, z3), (0, z4)]
    for k, g in ((1, g1), (2, g2), (3, g3)):
        ahead = xi >= k
        slots.append((jnp.where(ahead, 12 - k, 16 - k), g[0:toks, :]))
        slots.append((jnp.where(ahead, 8 - k, 12 - k), g[toks:2 * toks, :]))
    fill(lengths, first, slots, k_buf, v_buf)
    fill_queries(ends, first, q_ref, q_buf)
    lane = iota((rows, HEAD_DIM), 1)

    def finish(h, top, acc):
        ml = jnp.where(lane == 0, acc[:, HEAD_DIM:], top)
        for i in range(2):
            acc_ref[2 * h + i] = acc[i * toks:(i + 1) * toks, :HEAD_DIM]
            ml_ref[2 * h + i] = ml[i * toks:(i + 1) * toks]

    start = (lambda h: jnp.full((rows, HEAD_DIM), BIG, F32),
             lambda h, top, scale: jnp.zeros((rows, 2 * HEAD_DIM), F32))
    over_heads(pairs, len(slots), q_buf, k_buf, v_buf, s_a, s_b, 0, start, finish, False)


def attend_second_kernel(lengths, q_ref, g1, g2, g3, acc_ref, ml_ref, after, out_ref,
                         k_buf, v_buf, q_buf, s_a, s_b):
    pairs, rows = q_buf.shape[:2]
    toks = q_ref.shape[0]
    zi, xi = place_of()
    first = (zi * NX + xi) * toks
    ends = ends_of(lengths)
    slots = []
    for k, g in ((1, g1), (2, g2), (3, g3)):
        ahead = xi >= k
        slots.append((jnp.where(ahead, 16 - k, 4 - k), g[0:toks, :]))
        slots.append((jnp.where(ahead, 4 - k, 8 - k), g[toks:2 * toks, :]))
    fill(lengths, first, slots, k_buf, v_buf)
    fill_queries(ends, first, q_ref, q_buf)
    lane = iota((rows, HEAD_DIM), 1)

    def begin(h, top, scale):
        ml = two_of(ml_ref, h)
        old = jnp.exp2((ml[:, 1:2] - top) * scale)
        total = jnp.where(lane == 0, ml, 0.0)
        return jnp.concatenate([two_of(acc_ref, h), total], axis=1) * old

    def finish(h, top, acc):
        res = acc[:, :HEAD_DIM] / acc[:, HEAD_DIM:HEAD_DIM + 1]
        for i in range(2):
            out_ref[2 * h + i] = res[i * toks:(i + 1) * toks].astype(BF16)

    start = (lambda h: jnp.where(lane == 0, BIG, two_of(ml_ref, h)), begin)
    over_heads(pairs, len(slots), q_buf, k_buf, v_buf, s_a, s_b, None, start, finish, True)


def project_kernel(a_ref, w_ref, after, send_ref, keep_ref, wide, both):
    h = a_ref.shape[0]
    cols = both.shape[2]
    tp = lax.axis_index("tp")
    y, core = tp // 2, lax.rem(tp, 2)
    for i in range(h):
        wide[:, i * HEAD_DIM:(i + 1) * HEAD_DIM] = a_ref[i]
    for k in range(NY):
        at = pl.multiple_of(lax.rem(y + k, NY) * (2 * cols), 2 * cols)
        for c in range(2):
            both[c] = jnp.dot(wide[...], w_ref[:, pl.ds(at + c * cols, cols)], preferred_element_type=F32).astype(BF16)
        send_ref[k] = both[1 - core]
        keep_ref[k] = both[core]


def add_kernel(keep_ref, twin_ref, first_ref, *out_refs):
    first_ref[...] = keep_ref[0].astype(F32) + twin_ref[0].astype(F32)
    for k, out in enumerate(out_refs):
        out[...] = (keep_ref[k + 1].astype(F32) + twin_ref[k + 1].astype(F32)).astype(BF16)


def total_kernel(first_ref, a_ref, b_ref, c_ref, out_ref):
    total = first_ref[...] + a_ref[...].astype(F32)
    out_ref[...] = (total + b_ref[...].astype(F32) + c_ref[...].astype(F32)).astype(BF16)


def vmem(n):
    return [pl.BlockSpec(memory_space=pltpu.VMEM)] * n


def smem(n):
    return [pl.BlockSpec(memory_space=pltpu.SMEM)] * n


def cost(us):
    return pl.CostEstimate(flops=int(us * 1.1e9), transcendentals=0, bytes_accessed=int(us * 3.2e6))


def kept(shape, dtype):
    return pltpu.VMEM(shape, dtype)


def sds(shape, dtype):
    return jax.ShapeDtypeStruct(shape, dtype)


def far(a):
    return pltpu.with_memory_space_constraint(a, pltpu.HBM)


def params(mib):
    return pltpu.CompilerParams(vmem_limit_bytes=mib * 1024 * 1024)


def near(a):
    return pltpu.with_memory_space_constraint(a, pltpu.VMEM)


def x_shift(k):
    return [(NX * z + x, NX * z + (x + k) % NX) for z in range(NZ) for x in range(NX)]


def y_shift(k):
    return [(2 * y + c, 2 * ((y + k) % NY) + c) for y in range(NY) for c in range(2)]


def z_shift(k):
    return [(NX * z + x, NX * ((z + k) % NZ) + x) for z in range(NZ) for x in range(NX)]


TWIN = [(i, i ^ 1) for i in range(2 * NY)]


def body(mixer_input, gate_input, input_map, output_map, step_raw, step_bias, decay_log, skip_gain,
         norm_gain, queries, key_heads, value_heads, out_weight, rollout_lengths):
    toks, lanes = mixer_input.shape
    heads = step_raw.shape[0]
    msg = kept((STATE + EXTRA, QUARTER), BF16)
    quarter = kept((STATE, QUARTER), BF16)

    anywhere = [pl.BlockSpec(memory_space=pl.ANY)]
    chunk = kept((toks, 2 * HEAD_DIM), BF16)
    chunks = kept((2 * toks, 2 * HEAD_DIM), BF16)
    one = pl.BlockSpec(memory_space=pltpu.VMEM)
    o0, o1, o2, o3, own, dd, cumt, lead = pl.pallas_call(
        state_kernel,
        in_specs=smem(1) + vmem(7),
        out_specs=vmem(8),
        out_shape=[msg] * 4 + [chunk, kept((heads, toks), F32), kept((toks, heads), F32), kept((toks, heads), F32)],
        scratch_shapes=[pltpu.VMEM((NX, STATE + EXTRA, QUARTER), BF16)],
        compiler_params=params(12),
        cost_estimate=cost(30),
        name="chunk_states",
    )(*map(far, (rollout_lengths, mixer_input, input_map, step_raw, step_bias[None, :], decay_log[None, :],
                 key_heads, value_heads)))
    zs = [own, lax.ppermute(own, "ctx", z_shift(1))]
    came = [o0] + [lax.ppermute(o, "ctx", x_shift(k)) for k, o in ((1, o1), (2, o2), (3, o3))]

    y_local, token = pl.pallas_call(
        local_kernel,
        in_specs=smem(1) + vmem(6),
        out_specs=vmem(2),
        out_shape=[kept((toks, lanes), F32), kept((8, 128), F32)],
        scratch_shapes=[pltpu.VMEM((heads // 8, toks, 8), F32), pltpu.VMEM((heads // 8, 1, lanes * 8 // heads), F32)],
        compiler_params=params(12),
        cost_estimate=cost(25),
        name="within_chunk",
    )(rollout_lengths, near(mixer_input), near(input_map), near(output_map), *map(near, (dd, cumt)), skip_gain[None, :])

    sent = pl.pallas_call(
        relay_kernel, in_specs=vmem(1) + anywhere, out_specs=one, out_shape=chunk,
        compiler_params=params(4), cost_estimate=cost(5), name="relay",
    )(near(zs[1]), dd)
    for _ in range(3):
        sent = lax.ppermute(sent, "ctx", z_shift(1))
        zs.append(sent)
    soon = pl.pallas_call(
        join_kernel, in_specs=vmem(2), out_specs=one, out_shape=chunks,
        compiler_params=params(4), cost_estimate=cost(5), name="two_chunks",
    )(near(zs[1]), near(zs[2]))
    gs = [lax.ppermute(soon, "ctx", x_shift(k)) for k in (1, 2, 3)]
    prefix, total, pth = pl.pallas_call(
        row_kernel,
        in_specs=vmem(4) + [pl.BlockSpec(memory_space=pl.ANY)],
        out_specs=vmem(3),
        out_shape=[kept((NX, STATE, QUARTER), BF16), msg, kept((NX, 8, QUARTER), F32)],
        scratch_shapes=[pltpu.VMEM((NX, STATE + EXTRA, QUARTER), BF16)],
        compiler_params=params(8),
        cost_estimate=cost(10),
        name="row_scan",
    )(*map(near, came), token)

    once = lax.ppermute(total, "ctx", z_shift(1))
    pair = pl.pallas_call(
        pair_kernel,
        in_specs=vmem(2),
        out_specs=pl.BlockSpec(memory_space=pltpu.VMEM),
        out_shape=msg,
        compiler_params=params(4),
        cost_estimate=cost(5),
        name="two_rows",
    )(near(total), near(once))
    later = pl.pallas_call(
        edge_kernel, in_specs=vmem(3) + anywhere, out_specs=vmem(3), out_shape=[chunks] * 3,
        compiler_params=params(6), cost_estimate=cost(5), name="edge_chunks",
    )(near(own), near(zs[4]), near(zs[3]), pair)
    gs = gs + [lax.ppermute(a, "ctx", x_shift(k)) for k, a in zip((1, 2, 3), later)]

    twice = lax.ppermute(pair, "ctx", z_shift(1))
    before = lax.ppermute(twice, "ctx", z_shift(2))
    backs = pl.pallas_call(
        back_kernel,
        in_specs=vmem(4),
        out_specs=vmem(4),
        out_shape=[quarter] * 4,
        compiler_params=params(6),
        cost_estimate=cost(30),
        name="row_states",
    )(*map(near, (prefix, pth, twice, before)))
    incoming = [backs[0]] + [lax.ppermute(backs[k], "ctx", x_shift(k)) for k in (1, 2, 3)]

    q_heads = queries.shape[1] // HEAD_DIM
    acc, ml = pl.pallas_call(
        attend_first_kernel,
        in_specs=smem(1) + vmem(9) + anywhere,
        out_specs=vmem(2),
        out_shape=[kept((q_heads, toks, HEAD_DIM), F32)] * 2,
        scratch_shapes=attend_scratch(11, toks, q_heads),
        compiler_params=params(20),
        cost_estimate=cost(8),
        name="attend_first",
    )(rollout_lengths, queries, *map(near, (*zs, *gs[:3])), twice)
    attended = pl.pallas_call(
        attend_second_kernel,
        in_specs=smem(1) + vmem(6) + anywhere,
        out_specs=pl.BlockSpec(memory_space=pltpu.VMEM),
        out_shape=kept((q_heads, toks, HEAD_DIM), BF16),
        scratch_shapes=attend_scratch(6, toks, q_heads),
        compiler_params=params(14),
        cost_estimate=cost(5),
        name="attend_second",
    )(rollout_lengths, queries, *map(near, (*gs[3:], acc, ml)), twice)

    cols = out_weight.shape[1] // (2 * NY)
    send, keep = pl.pallas_call(
        project_kernel,
        in_specs=vmem(2) + anywhere,
        out_specs=vmem(2),
        out_shape=[kept((NY, toks, cols), BF16)] * 2,
        scratch_shapes=[pltpu.VMEM((toks, q_heads * HEAD_DIM), BF16), pltpu.VMEM((2, toks, cols), BF16)],
        compiler_params=params(8),
        cost_estimate=cost(3),
        name="project",
    )(near(attended), near(out_weight), pair)
    twin = lax.ppermute(send, "tp", TWIN)
    part = kept((toks, cols), BF16)
    mine, *summed = pl.pallas_call(
        add_kernel, in_specs=vmem(2), out_specs=vmem(NY), out_shape=[kept((toks, cols), F32)] + [part] * (NY - 1),
        compiler_params=params(6), cost_estimate=cost(0.5), name="two_cores",
    )(near(keep), near(twin))
    others = [lax.ppermute(a, "tp", y_shift(k)) for k, a in zip((1, 2, 3), summed)]
    block_out = pl.pallas_call(
        total_kernel, in_specs=vmem(NY), out_specs=one, out_shape=sds((toks, cols), BF16),
        compiler_params=params(6), cost_estimate=cost(0.5), name="four_rows",
    )(*map(near, (mine, *others)))

    mamba_out = pl.pallas_call(
        gate_kernel,
        in_specs=vmem(9),
        out_specs=pl.BlockSpec(memory_space=pltpu.VMEM),
        out_shape=sds((toks, lanes), BF16),
        scratch_shapes=[pltpu.VMEM((NX, STATE, QUARTER), BF16)],
        compiler_params=params(12),
        cost_estimate=cost(2.5),
        name="carry_gate_norm",
    )(*map(near, (y_local, output_map, lead, gate_input)), norm_gain[None, :], *map(near, incoming))
    return (mamba_out, block_out)


def solution(mesh):
    both = P("ctx", "tp")
    return jax.shard_map(
        body,
        mesh=mesh,
        in_specs=(both, both, both, both, P("tp", "ctx"), P("tp"), P("tp"), P("tp"), P("tp"),
                  both, both, both, P("tp", None), P()),
        out_specs=(both, both),
        check_vma=False,
    )
```
